512 devices in a mesh: row: 32 (over z, x), col: 16 (over y, core).
Axes of the slice: x: 4, y: 8, z: 8, core: 2. Of those that a mesh axis runs over, the one named last changes fastest.
Arguments:
- images: bfloat16 [4096, 1152], P('row'), may hold values from -4 to 4
- captions: bfloat16 [32768, 1152], P('col'), may hold values from -4 to 4
Outputs:
- image_dual: float32 [4096], P('row')
- caption_dual: float32 [32768], P('col')
- mapped: float32 [4096, 1152], P('row', 'col')
The draws below stay inside these ranges and needn't reach their ends.
All inputs are finite; a program needn't handle non-finite values.
Results may differ from the reference program's by a relative error of at most 0.0023.
Values sent between devices are 32-bit elements; how exact they have to be, the bound alone decides.
A program may use at most 64 MiB of HBM per device.

```python
import math
import jax
import jax.numpy as jnp
from jax import lax

D = 1152
TI = 128
ITERS = 2
NI = 4096
NC = 32768


def draw_images(key, part):
    key = jax.random.fold_in(key, 1)
    key_rows, key_scale = jax.random.split(key, 2)
    rows = jax.random.normal(key_rows, (NI, D), jnp.float32) / math.sqrt(D)
    scale = jnp.exp(jax.random.uniform(key_scale, (NI, 1), jnp.float32, math.log(0.6), math.log(6.0)))
    values = rows * scale
    return values.astype(jnp.bfloat16)


def draw_captions(key, part):
    key = jax.random.fold_in(key, 2)
    key_rows, key_scale = jax.random.split(key, 2)
    rows = jax.random.normal(key_rows, (NC, D), jnp.float32) / math.sqrt(D)
    scale = jnp.exp(jax.random.uniform(key_scale, (NC, 1), jnp.float32, math.log(0.6), math.log(6.0)))
    values = rows * scale
    return values.astype(jnp.bfloat16)


def setup_inputs(seed: int = 0) -> dict:
    key_list = jax.random.split(jax.random.key(seed), 3)
    return {
        "images": draw_images(jax.random.fold_in(key_list[2], 71), 0),
        "captions": draw_captions(jax.random.fold_in(key_list[2], 71), 0),
    }


entropic = 0.05


def similarity(block, captions):
    return lax.dot_general(block, captions, (((1,), (1,)), ((), ())), preferred_element_type=jnp.float32)


def reference(images, captions):
    blocks = images.reshape(NI // TI, TI, D)
    log_a = jnp.float32(-math.log(NI))
    log_b = jnp.float32(-math.log(NC))
    caption_dual = jnp.zeros((NC,), jnp.float32)
    image_dual = jnp.zeros((NI,), jnp.float32)
    for step in range(ITERS):
        def row_update(block):
            logits = (caption_dual[None, :] + similarity(block, captions)) / entropic
            top = jnp.max(logits, axis=1)
            total = jnp.sum(jnp.exp(logits - top[:, None]), axis=1)
            return entropic * log_a - entropic * (top + jnp.log(total))

        image_dual = lax.map(row_update, blocks).reshape(NI)

        def column_step(carry, inputs):
            run_max, run_sum = carry
            block, duals = inputs
            logits = (duals[:, None] + similarity(block, captions)) / entropic
            new_max = jnp.maximum(run_max, jnp.max(logits, axis=0))
            new_sum = run_sum * jnp.exp(run_max - new_max) + jnp.sum(jnp.exp(logits - new_max[None, :]), axis=0)
            return (new_max, new_sum), None

        start = (jnp.full((NC,), -1e30, jnp.float32), jnp.zeros((NC,), jnp.float32))
        (col_max, col_sum), unused = lax.scan(column_step, start, (blocks, image_dual.reshape(NI // TI, TI)))
        caption_dual = entropic * log_b - entropic * (col_max + jnp.log(col_sum))

    def final_map(block):
        logits = (caption_dual[None, :] + similarity(block, captions)) / entropic
        top = jnp.max(logits, axis=1)
        weights = jnp.exp(logits - top[:, None])
        mass = jnp.sum(weights, axis=1)
        numer = jnp.dot(weights.astype(jnp.bfloat16), captions, preferred_element_type=jnp.float32)
        return numer / mass[:, None]

    mapped = lax.map(final_map, blocks).reshape(NI, D)
    return image_dual, caption_dual, mapped
```

```python
import functools
import math

import jax
import jax.numpy as jnp
from jax import lax
from jax.experimental import pallas as pl
from jax.experimental.pallas import tpu as pltpu
from jax.sharding import PartitionSpec as P

MESH = pl.DeviceIdType.MESH
ENTROPIC = 0.05
LOG2E = math.log2(math.e)
ITERS = 2
LANES = 128
GROUP = 16
X_CHIPS = 4


def ring(offset, size):
    return min(offset, size - offset)


def tree(op, values):
    values = list(values)
    while len(values) > 1:
        rest = [op(a, b) for a, b in zip(values[::2], values[1::2])]
        values = rest + ([values[-1]] if len(values) % 2 else [])
    return values[0]


def lse_of(parts):
    top = tree(jnp.maximum, parts)
    return top + jnp.log2(tree(jnp.add, [jnp.exp2(p - top) for p in parts]))


def kernel(
    rows_n, cols_n, images_hbm, captions_hbm, image_out, caption_out, mapped_out,
    images, captions, score, weights, stat_max, stat_sum, block_max, block_sum, dual,
    image_src, image_recv, caption_src, caption_recv, numer, pair_recv, y_src, y_recv,
    load_sem, image_ssem, image_rsem, caption_ssem, caption_rsem,
    pair_ssem, pair_rsem, y_ssem, y_rsem,
):
    here, width = images.shape
    blocks = score.shape[1] // LANES
    loads = captions.shape[0] // 256
    x_n = X_CHIPS
    z_n = rows_n // x_n
    y_n = cols_n // 2
    share = width // cols_n
    r, c = lax.axis_index("row"), lax.axis_index("col")
    z, x, y, core = r // x_n, lax.rem(r, x_n), c // 2, lax.rem(c, 2)

    def row_peer(dz, dx):
        return (lax.rem(z + dz, z_n) * x_n + lax.rem(x + dx, x_n), c)

    def col_peer(dy, dc):
        return (r, lax.rem(y + dy, y_n) * 2 + lax.rem(core + dc, 2))

    row_peers = sorted(
        [(dz, dx) for dz in range(z_n) for dx in range(x_n) if dz or dx],
        key=lambda p: -ring(p[0], z_n) - ring(p[1], x_n),
    )
    col_peers = sorted(
        [(dy, dc) for dy in range(y_n) for dc in range(2) if dy or dc],
        key=lambda p: -ring(p[0], y_n) - 0.5 * p[1],
    )
    y_peers = sorted(range(1, y_n), key=lambda p: -ring(p, y_n))

    image_load = pltpu.make_async_copy(images_hbm, images, load_sem.at[loads])
    image_load.start()
    caption_loads = []
    for b in range(loads):
        part = pl.ds(b * 256, 256)
        caption_loads.append(
            pltpu.make_async_copy(captions_hbm.at[part], captions.at[part], load_sem.at[b])
        )
        caption_loads[-1].start()

    barrier = pltpu.get_barrier_semaphore()
    for p in row_peers:
        pl.semaphore_signal(barrier, inc=1, device_id=row_peer(*p), device_id_type=MESH)
    for p in col_peers:
        pl.semaphore_signal(barrier, inc=1, device_id=col_peer(*p), device_id_type=MESH)

    image_load.wait()
    for b in range(loads):
        caption_loads[b].wait()
        part = pl.ds(b * 256, 256)
        score[:, part] = lax.dot_general(
            images[...], captions[part, :], (((1,), (1,)), ((), ())),
            preferred_element_type=jnp.float32,
        ) * jnp.float32(LOG2E / ENTROPIC)

    log_a = jnp.float32(-math.log2(here * rows_n))
    log_b = jnp.float32(-math.log2(score.shape[1] * cols_n))

    def logit_rows(g, with_dual):
        rows = pl.ds(g * GROUP, GROUP)
        out = []
        for b in range(blocks):
            v = score[rows, pl.ds(b * LANES, LANES)]
            out.append(v + dual[pl.ds(b, 1), :] if with_dual else v)
        return rows, out

    def send_image(step):
        for k, p in enumerate(col_peers):
            pltpu.make_async_remote_copy(
                src_ref=image_src.at[step], dst_ref=image_recv.at[step, k],
                send_sem=image_ssem.at[step], recv_sem=image_rsem.at[step],
                device_id=col_peer(*p), device_id_type=MESH,
            ).start()

    def get_image(step):
        whole = image_recv.at[step]
        pltpu.make_async_copy(whole, whole, image_rsem.at[step]).wait()
        return lse_of(
            [image_src[step]] + [image_recv[step, k] for k in range(len(col_peers))]
        )

    for step in range(ITERS):
        for g in range(here // GROUP):
            rows, logits = logit_rows(g, step > 0)
            top = tree(jnp.maximum, logits)
            stat_max[rows, :] = top
            stat_sum[rows, :] = tree(jnp.add, [jnp.exp2(v - top) for v in logits])
        lane_max = stat_max[...].T
        top = jnp.max(lane_max, axis=0, keepdims=True)
        total = jnp.sum(stat_sum[...].T * jnp.exp2(lane_max - top), axis=0, keepdims=True)
        image_src[step] = top + jnp.log2(total)
        if step == 0:
            pl.semaphore_wait(barrier, len(row_peers) + len(col_peers))
        send_image(step)
        image_dual = log_a - get_image(step)
        if step == ITERS - 1:
            image_out[...] = image_dual * jnp.float32(ENTROPIC / LOG2E)
        column = jnp.broadcast_to(image_dual, (LANES, here)).T
        for b in range(blocks):
            logits = score[:, pl.ds(b * LANES, LANES)] + column
            top = jnp.max(logits, axis=0, keepdims=True)
            block_max[pl.ds(b, 1), :] = top
            block_sum[pl.ds(b, 1), :] = jnp.sum(jnp.exp2(logits - top), axis=0, keepdims=True)
        caption_src[step] = block_max[...] + jnp.log2(block_sum[...])
        for k, p in enumerate(row_peers):
            pltpu.make_async_remote_copy(
                src_ref=caption_src.at[step], dst_ref=caption_recv.at[step, k],
                send_sem=caption_ssem.at[step], recv_sem=caption_rsem.at[step],
                device_id=row_peer(*p), device_id_type=MESH,
            ).start()
        whole = caption_recv.at[step]
        pltpu.make_async_copy(whole, whole, caption_rsem.at[step]).wait()
        dual[...] = log_b - lse_of(
            [caption_src[step]] + [caption_recv[step, k] for k in range(len(row_peers))]
        )

    caption_out[...] = dual[...] * jnp.float32(ENTROPIC / LOG2E)
    for g in range(here // GROUP):
        rows, logits = logit_rows(g, True)
        top = jnp.max(tree(jnp.maximum, logits), axis=1, keepdims=True)
        stat_max[rows, :] = jnp.broadcast_to(top, (GROUP, LANES))
        terms = [jnp.exp2(v - top) for v in logits]
        stat_sum[rows, :] = tree(jnp.add, terms)
        for b, w in enumerate(terms):
            weights[rows, pl.ds(b * LANES, LANES)] = w.astype(jnp.bfloat16)
    own_top = stat_max[...].T[0:1, :]
    mass = jnp.sum(stat_sum[...].T, axis=0, keepdims=True)
    image_src[ITERS] = own_top + jnp.log2(mass)
    send_image(ITERS)

    for b in range(width // LANES):
        part = pl.ds(b * LANES, LANES)
        numer[part, :] = jnp.dot(
            weights[...], captions[:, part], preferred_element_type=jnp.float32
        ).T
    factor = jnp.exp2(own_top - get_image(ITERS))

    def chunk(dy, of_core):
        start = (lax.rem(y + dy, y_n) * 2 + of_core) * share
        return pl.ds(pl.multiple_of(start, 8), share)

    pair_order = y_peers + [0]
    for dy in pair_order:
        part = chunk(dy, 1 - core)
        numer[part, :] = numer[part, :] * factor
        pltpu.make_async_remote_copy(
            src_ref=numer.at[part], dst_ref=pair_recv.at[dy],
            send_sem=pair_ssem, recv_sem=pair_rsem.at[dy],
            device_id=col_peer(0, 1), device_id_type=MESH,
        ).start()
    copies = []
    for dy in pair_order:
        pltpu.make_async_copy(pair_recv.at[dy], pair_recv.at[dy], pair_rsem.at[dy]).wait()
        y_src[dy] = numer[chunk(dy, core), :] * factor + pair_recv[dy]
        if dy:
            copies.append(
                pltpu.make_async_remote_copy(
                    src_ref=y_src.at[dy], dst_ref=y_recv.at[dy - 1],
                    send_sem=y_ssem, recv_sem=y_rsem.at[dy - 1],
                    device_id=col_peer(dy, 0), device_id_type=MESH,
                )
            )
            copies[-1].start()
    total = y_src[0]
    for dy in reversed(y_peers):
        pltpu.make_async_copy(y_recv.at[dy - 1], y_recv.at[dy - 1], y_rsem.at[dy - 1]).wait()
        total = total + y_recv[dy - 1]
    mapped_out[...] = total

    for step in range(ITERS + 1):
        whole = image_recv.at[step]
        pltpu.make_async_copy(whole, whole, image_ssem.at[step]).wait()
    for step in range(ITERS):
        whole = caption_recv.at[step]
        pltpu.make_async_copy(whole, whole, caption_ssem.at[step]).wait()
    pltpu.make_async_copy(pair_recv, pair_recv, pair_ssem).wait()
    pltpu.make_async_copy(y_recv, y_recv, y_ssem).wait()


def solution(mesh):
    rows_n, cols_n = mesh.shape["row"], mesh.shape["col"]
    y_n = cols_n // 2

    def per_device(images, captions):
        here, width = images.shape
        cols = captions.shape[0]
        share = width // cols_n
        blocks = cols // LANES
        f32 = jnp.float32
        vmem = pl.BlockSpec(memory_space=pltpu.VMEM)
        dma = pltpu.SemaphoreType.DMA
        image_dual, caption_dual, mapped = pl.pallas_call(
            functools.partial(kernel, rows_n, cols_n),
            out_shape=(
                jax.ShapeDtypeStruct((1, here), f32),
                jax.ShapeDtypeStruct((blocks, LANES), f32),
                jax.ShapeDtypeStruct((share, here), f32),
            ),
            in_specs=[pl.BlockSpec(memory_space=pl.ANY)] * 2,
            out_specs=(vmem, vmem, vmem),
            scratch_shapes=[
                pltpu.VMEM((here, width), jnp.bfloat16),
                pltpu.VMEM((cols, width), jnp.bfloat16),
                pltpu.VMEM((here, cols), f32),
                pltpu.VMEM((here, cols), jnp.bfloat16),
                pltpu.VMEM((here, LANES), f32),
                pltpu.VMEM((here, LANES), f32),
                pltpu.VMEM((blocks, LANES), f32),
                pltpu.VMEM((blocks, LANES), f32),
                pltpu.VMEM((blocks, LANES), f32),
                pltpu.VMEM((ITERS + 1, 1, here), f32),
                pltpu.VMEM((ITERS + 1, cols_n - 1, 1, here), f32),
                pltpu.VMEM((ITERS, blocks, LANES), f32),
                pltpu.VMEM((ITERS, rows_n - 1, blocks, LANES), f32),
                pltpu.VMEM((width, here), f32),
                pltpu.VMEM((y_n, share, here), f32),
                pltpu.VMEM((y_n, share, here), f32),
                pltpu.VMEM((y_n - 1, share, here), f32),
                dma((cols // 256 + 1,)),
                dma((ITERS + 1,)),
                dma((ITERS + 1,)),
                dma((ITERS,)),
                dma((ITERS,)),
                dma,
                dma((y_n,)),
                dma,
                dma((y_n - 1,)),
            ],
            compiler_params=pltpu.CompilerParams(
                collective_id=0, has_side_effects=True, vmem_limit_bytes=60 * 2**20
            ),
            name="sinkhorn",
        )(images, captions)
        return image_dual.reshape(here), caption_dual.reshape(cols), mapped.T

    return jax.shard_map(
        per_device,
        mesh=mesh,
        in_specs=(P("row", None), P("col", None)),
        out_specs=(P("row"), P("col"), P("row", "col")),
        check_vma=False,
    )
```

```python
import functools
import math

import jax
import jax.numpy as jnp
from jax import lax
from jax.experimental import pallas as pl
from jax.experimental.pallas import tpu as pltpu
from jax.sharding import PartitionSpec as P

MESH = pl.DeviceIdType.MESH
ENTROPIC = 0.05
LOG2E = math.log2(math.e)
ITERS = 2
LANES = 128
GROUP = 16
CHUNK = 512
X_CHIPS = 4


def ring(offset, size):
    return min(offset, size - offset)


def tree(op, values):
    values = list(values)
    while len(values) > 1:
        rest = [op(a, b) for a, b in zip(values[::2], values[1::2])]
        values = rest + ([values[-1]] if len(values) % 2 else [])
    return values[0]


def lse_of(parts):
    top = tree(jnp.maximum, parts)
    return top + jnp.log2(tree(jnp.add, [jnp.exp2(p - top) for p in parts]))


def send(src, dst, ssem, rsem, device):
    pltpu.make_async_remote_copy(
        src_ref=src, dst_ref=dst, send_sem=ssem, recv_sem=rsem,
        device_id=device, device_id_type=MESH,
    ).start()


def drain(ref, sem):
    pltpu.make_async_copy(ref, ref, sem).wait()


def greet(barrier, device):
    pl.semaphore_signal(barrier, inc=1, device_id=device, device_id_type=MESH)


def kernel(
    rows_n, cols_n, images_hbm, captions_hbm, image_out, caption_out, mapped_out,
    images, captions, score, weights, stat_max, stat_sum, block_max, block_sum, dual,
    image_src, image_recv, caption_src, caption_recv, tail_src, tail_recv, numer, pair_recv, y_src, y_recv,
    load_sem, image_ssem, image_rsem, caption_ssem, caption_rsem, tail_ssem, tail_rsem,
    pair_ssem, pair_rsem, y_ssem, y_rsem,
):
    here, width = images.shape
    blocks = score.shape[1] // LANES
    loads = captions.shape[0] // CHUNK
    x_n = X_CHIPS
    z_n = rows_n // x_n
    y_n = cols_n // 2
    share = width // cols_n
    r, c = lax.axis_index("row"), lax.axis_index("col")
    z, x, y, core = r // x_n, lax.rem(r, x_n), c // 2, lax.rem(c, 2)

    def row_peer(dz, dx):
        return (lax.rem(z + dz, z_n) * x_n + lax.rem(x + dx, x_n), c)

    def col_peer(dy, dc):
        return (r, lax.rem(y + dy, y_n) * 2 + lax.rem(core + dc, 2))

    row_peers = sorted(
        [(dz, dx) for dz in range(z_n) for dx in range(x_n) if dz or dx],
        key=lambda p: -ring(p[0], z_n) - ring(p[1], x_n),
    )
    col_peers = sorted(
        [(dy, dc) for dy in range(y_n) for dc in range(2) if dy or dc],
        key=lambda p: (p[0] > 0, -ring(p[0], y_n), p[1]),
    )
    first = y_n // 4
    made = [(first + q) % y_n for q in range(y_n)]
    y_order = sorted(range(y_n), key=lambda p: (-ring(p, y_n), made.index(p)))

    image_load = pltpu.make_async_copy(images_hbm, images, load_sem.at[loads])
    image_load.start()
    caption_loads = []
    for b in range(loads):
        part = pl.ds(b * CHUNK, CHUNK)
        caption_loads.append(
            pltpu.make_async_copy(captions_hbm.at[part], captions.at[part], load_sem.at[b])
        )
        caption_loads[-1].start()

    barrier = pltpu.get_barrier_semaphore()
    for p in row_peers:
        greet(barrier, row_peer(*p))
    for p in col_peers:
        greet(barrier, col_peer(*p))

    image_load.wait()
    for b in range(loads):
        caption_loads[b].wait()
        part = pl.ds(b * CHUNK, CHUNK)
        score[:, part] = lax.dot_general(
            images[...], captions[part, :], (((1,), (1,)), ((), ())),
            preferred_element_type=jnp.float32,
        ) * jnp.float32(LOG2E / ENTROPIC)
        for g in range(here // GROUP):
            rows = pl.ds(g * GROUP, GROUP)
            logits = [
                score[rows, pl.ds(b * CHUNK + i * LANES, LANES)] for i in range(CHUNK // LANES)
            ]
            top = tree(jnp.maximum, logits)
            if b:
                old = stat_max[rows, :]
                top = jnp.maximum(top, old)
            total = tree(jnp.add, [jnp.exp2(v - top) for v in logits])
            if b:
                total = total + stat_sum[rows, :] * jnp.exp2(old - top)
            stat_max[rows, :] = top
            stat_sum[rows, :] = total

    log_a = jnp.float32(-math.log2(here * rows_n))
    log_b = jnp.float32(-math.log2(score.shape[1] * cols_n))

    def logit_rows(g):
        rows = pl.ds(g * GROUP, GROUP)
        return rows, [
            score[rows, pl.ds(b * LANES, LANES)] + dual[pl.ds(b, 1), :] for b in range(blocks)
        ]

    def send_image(step):
        for k, p in enumerate(col_peers):
            send(
                image_src.at[step], image_recv.at[step, k],
                image_ssem.at[step], image_rsem.at[step], col_peer(*p),
            )

    def get_image(step):
        drain(image_recv.at[step], image_rsem.at[step])
        return lse_of(
            [image_src[step]] + [image_recv[step, k] for k in range(len(col_peers))]
        )

    for step in range(ITERS):
        for g in range(here // GROUP if step else 0):
            rows, logits = logit_rows(g)
            top = tree(jnp.maximum, logits)
            stat_max[rows, :] = top
            stat_sum[rows, :] = tree(jnp.add, [jnp.exp2(v - top) for v in logits])
        lane_max = stat_max[...].T
        top = jnp.max(lane_max, axis=0, keepdims=True)
        total = jnp.sum(stat_sum[...].T * jnp.exp2(lane_max - top), axis=0, keepdims=True)
        image_src[step] = top + jnp.log2(total)
        if step == 0:
            pl.semaphore_wait(barrier, len(row_peers) + len(col_peers))
        send_image(step)
        image_dual = log_a - get_image(step)
        if step == ITERS - 1:
            image_out[...] = image_dual * jnp.float32(ENTROPIC / LOG2E)
        column = jnp.broadcast_to(image_dual, (LANES, here)).T
        for b in range(blocks):
            logits = score[:, pl.ds(b * LANES, LANES)] + column
            top = jnp.max(logits, axis=0, keepdims=True)
            block_max[pl.ds(b, 1), :] = top
            block_sum[pl.ds(b, 1), :] = jnp.sum(jnp.exp2(logits - top), axis=0, keepdims=True)
        caption_src[step] = block_max[...] + jnp.log2(block_sum[...])
        for k, p in enumerate(row_peers):
            send(
                caption_src.at[step], caption_recv.at[step, k],
                caption_ssem.at[step], caption_rsem.at[step], row_peer(*p),
            )
        drain(caption_recv.at[step], caption_rsem.at[step])
        dual[...] = log_b - lse_of(
            [caption_src[step]] + [caption_recv[step, k] for k in range(len(row_peers))]
        )

    caption_out[...] = dual[...] * jnp.float32(ENTROPIC / LOG2E)
    for g in range(here // GROUP):
        rows, logits = logit_rows(g)
        top = jnp.max(tree(jnp.maximum, logits), axis=1, keepdims=True)
        stat_max[rows, :] = jnp.broadcast_to(top, (GROUP, LANES))
        terms = [jnp.exp2(v - top) for v in logits]
        stat_sum[rows, :] = tree(jnp.add, terms)
        for b, w in enumerate(terms):
            weights[rows, pl.ds(b * LANES, LANES)] = w.astype(jnp.bfloat16)
    tail_src[0:1, :] = stat_max[...].T[0:1, :]
    tail_src[1:2, :] = jnp.sum(stat_sum[...].T, axis=0, keepdims=True)
    for k, p in enumerate(col_peers):
        send(tail_src, tail_recv.at[k], tail_ssem, tail_rsem.at[min(k, 1)], col_peer(*p))

    def chunk(dy, of_core):
        start = (lax.rem(y + dy, y_n) * 2 + of_core) * share
        return pl.ds(pl.multiple_of(start, 8), share)

    width_blocks = width // LANES
    reach = [0]
    for q in range(y_n):
        ends = [(2 * share * at) % LANES + 2 * share * (q + 1) for at in range(y_n)]
        reach.append(min(width_blocks, -(-max(ends) // LANES)))
    start = 2 * share * lax.rem(y + first, y_n) // LANES
    for q, dy in enumerate(made):
        for i in range(reach[q], reach[q + 1]):
            block = lax.rem(start + i, width_blocks) * LANES
            part = pl.ds(pl.multiple_of(block, LANES), LANES)
            numer[part, :] = jnp.dot(
                weights[...], captions[:, part], preferred_element_type=jnp.float32
            ).T
        part = chunk(dy, 1 - core)
        send(numer.at[part], pair_recv.at[dy], pair_ssem, pair_rsem.at[dy], col_peer(0, 1))

    drain(tail_recv.at[0], tail_rsem.at[0])
    own_top, other_top = tail_src[0:1, :], tail_recv[0, 0:1, :]
    pair_top = jnp.maximum(own_top, other_top)
    own_scale, other_scale = jnp.exp2(own_top - pair_top), jnp.exp2(other_top - pair_top)
    for dy in y_order:
        drain(pair_recv.at[dy], pair_rsem.at[dy])
        y_src[dy] = numer[chunk(dy, core), :] * own_scale + pair_recv[dy] * other_scale
        if dy:
            send(y_src.at[dy], y_recv.at[dy - 1], y_ssem, y_rsem.at[dy - 1], col_peer(dy, 0))

    rest = tail_recv.at[pl.ds(1, len(col_peers) - 1)]
    drain(rest, tail_rsem.at[1])
    senders = [((y_n - dy) % y_n, dc) for dy, dc in col_peers]
    tops = {p: tail_recv[k, 0:1, :] for k, p in enumerate(senders)}
    masses = {p: tail_recv[k, 1:2, :] for k, p in enumerate(senders)}
    tops[0, 0], masses[0, 0] = own_top, tail_src[1:2, :]
    top = tree(jnp.maximum, list(tops.values()))
    mass = tree(jnp.add, [masses[p] * jnp.exp2(tops[p] - top) for p in tops])
    inverse = 1.0 / mass
    factor = [
        jnp.exp2(jnp.maximum(tops[dy, 0], tops[dy, 1]) - top) * inverse for dy in range(y_n)
    ]
    total = y_src[0] * factor[0]
    for dy in sorted(range(1, y_n), key=lambda p: ring(p, y_n)):
        sender = y_n - dy
        drain(y_recv.at[dy - 1], y_rsem.at[dy - 1])
        total = total + y_recv[dy - 1] * factor[sender]
    mapped_out[...] = total

    for step in range(ITERS):
        drain(image_recv.at[step], image_ssem.at[step])
    drain(tail_recv, tail_ssem)
    for step in range(ITERS):
        drain(caption_recv.at[step], caption_ssem.at[step])
    drain(pair_recv, pair_ssem)
    drain(y_recv, y_ssem)


def place(image_dual, caption_dual, mapped, image_out, caption_out, mapped_out, sems):
    pairs = ((mapped, mapped_out), (caption_dual, caption_out), (image_dual, image_out))
    copies = [pltpu.make_async_copy(a, b, sems.at[i]) for i, (a, b) in enumerate(pairs)]
    for copy in copies:
        copy.start()
    for copy in copies:
        copy.wait()


def solution(mesh):
    rows_n, cols_n = mesh.shape["row"], mesh.shape["col"]
    y_n = cols_n // 2

    def per_device(images, captions):
        here, width = images.shape
        cols = captions.shape[0]
        share = width // cols_n
        blocks = cols // LANES
        f32 = jnp.float32
        vmem = pl.BlockSpec(memory_space=pltpu.VMEM)
        dma = pltpu.SemaphoreType.DMA
        shapes = ((1, here), (blocks, LANES), (share, here))
        parts = pl.pallas_call(
            functools.partial(kernel, rows_n, cols_n),
            out_shape=tuple(pltpu.VMEM(shape, f32) for shape in shapes),
            in_specs=[pl.BlockSpec(memory_space=pl.ANY)] * 2,
            out_specs=(vmem, vmem, vmem),
            scratch_shapes=[
                pltpu.VMEM((here, width), jnp.bfloat16),
                pltpu.VMEM((cols, width), jnp.bfloat16),
                pltpu.VMEM((here, cols), f32),
                pltpu.VMEM((here, cols), jnp.bfloat16),
                pltpu.VMEM((here, LANES), f32),
                pltpu.VMEM((here, LANES), f32),
                pltpu.VMEM((blocks, LANES), f32),
                pltpu.VMEM((blocks, LANES), f32),
                pltpu.VMEM((blocks, LANES), f32),
                pltpu.VMEM((ITERS, 1, here), f32),
                pltpu.VMEM((ITERS, cols_n - 1, 1, here), f32),
                pltpu.VMEM((ITERS, blocks, LANES), f32),
                pltpu.VMEM((ITERS, rows_n - 1, blocks, LANES), f32),
                pltpu.VMEM((2, here), f32),
                pltpu.VMEM((cols_n - 1, 2, here), f32),
                pltpu.VMEM((width, here), f32),
                pltpu.VMEM((y_n, share, here), f32),
                pltpu.VMEM((y_n, share, here), f32),
                pltpu.VMEM((y_n - 1, share, here), f32),
                dma((cols // CHUNK + 1,)),
                dma((ITERS,)),
                dma((ITERS,)),
                dma((ITERS,)),
                dma((ITERS,)),
                dma,
                dma((2,)),
                dma,
                dma((y_n,)),
                dma,
                dma((y_n - 1,)),
            ],
            compiler_params=pltpu.CompilerParams(
                collective_id=0, has_side_effects=True, vmem_limit_bytes=60 * 2**20
            ),
            name="sinkhorn",
        )(images, captions)
        image_dual, caption_dual, mapped = pl.pallas_call(
            place,
            out_shape=tuple(jax.ShapeDtypeStruct(shape, f32) for shape in shapes),
            in_specs=[vmem] * 3,
            out_specs=[pl.BlockSpec(memory_space=pl.ANY)] * 3,
            scratch_shapes=[dma((3,))],
            name="place",
        )(*[pltpu.with_memory_space_constraint(p, pltpu.VMEM) for p in parts])
        return image_dual.reshape(here), caption_dual.reshape(cols), mapped.T

    return jax.shard_map(
        per_device,
        mesh=mesh,
        in_specs=(P("row", None), P("col", None)),
        out_specs=(P("row"), P("col"), P("row", "col")),
        check_vma=False,
    )
```

```python
import functools
import math

import jax
import jax.numpy as jnp
from jax import lax
from jax.experimental import pallas as pl
from jax.experimental.pallas import tpu as pltpu
from jax.sharding import PartitionSpec as P

MESH = pl.DeviceIdType.MESH
ENTROPIC = 0.05
LOG2E = math.log2(math.e)
ITERS = 2
LANES = 128
GROUP = 16
CHUNK = 512
X_CHIPS = 4


def ring(offset, size):
    return min(offset, size - offset)


def tree(op, values):
    values = list(values)
    while len(values) > 1:
        rest = [op(a, b) for a, b in zip(values[::2], values[1::2])]
        values = rest + ([values[-1]] if len(values) % 2 else [])
    return values[0]


def lse_of(parts):
    top = tree(jnp.maximum, parts)
    return top + jnp.log2(tree(jnp.add, [jnp.exp2(p - top) for p in parts]))


def send(src, dst, ssem, rsem, device):
    pltpu.make_async_remote_copy(
        src_ref=src, dst_ref=dst, send_sem=ssem, recv_sem=rsem,
        device_id=device, device_id_type=MESH,
    ).start()


def drain(ref, sem):
    pltpu.make_async_copy(ref, ref, sem).wait()


def greet(barrier, device):
    pl.semaphore_signal(barrier, inc=1, device_id=device, device_id_type=MESH)


def kernel(
    rows_n, cols_n, images_hbm, captions_hbm, image_out, caption_out, mapped_out,
    images, captions, score, weights, stat_max, stat_sum, block_max, block_sum, dual,
    image_src, image_recv, caption_src, caption_recv, tail_src, tail_recv, numer, pair_recv, y_src, y_recv,
    load_sem, image_ssem, image_rsem, caption_ssem, caption_rsem, tail_ssem, tail_rsem,
    pair_ssem, pair_rsem, y_ssem, y_rsem,
):
    here, width = images.shape
    blocks = score.shape[1] // LANES
    loads = captions.shape[0] // CHUNK
    x_n = X_CHIPS
    z_n = rows_n // x_n
    y_n = cols_n // 2
    share = width // cols_n
    r, c = lax.axis_index("row"), lax.axis_index("col")
    z, x, y, core = r // x_n, lax.rem(r, x_n), c // 2, lax.rem(c, 2)

    def row_peer(dz, dx):
        return (lax.rem(z + dz, z_n) * x_n + lax.rem(x + dx, x_n), c)

    def col_peer(dy, dc):
        return (r, lax.rem(y + dy, y_n) * 2 + lax.rem(core + dc, 2))

    row_peers = sorted(
        [(dz, dx) for dz in range(z_n) for dx in range(x_n) if dz or dx],
        key=lambda p: -ring(p[0], z_n) - ring(p[1], x_n),
    )
    col_peers = sorted(
        [(dy, dc) for dy in range(y_n) for dc in range(2) if dy or dc],
        key=lambda p: (p[0] > 0, -ring(p[0], y_n), p[1]),
    )
    y_order = list(range(y_n // 2)) + list(range(y_n // 2, y_n))[::-1]

    image_load = pltpu.make_async_copy(images_hbm, images, load_sem.at[loads])
    image_load.start()
    caption_loads = []
    for b in range(loads):
        part = pl.ds(b * CHUNK, CHUNK)
        caption_loads.append(
            pltpu.make_async_copy(captions_hbm.at[part], captions.at[part], load_sem.at[b])
        )
        caption_loads[-1].start()

    barrier = pltpu.get_barrier_semaphore()
    for p in row_peers:
        greet(barrier, row_peer(*p))
    for p in col_peers:
        greet(barrier, col_peer(*p))

    image_load.wait()
    for b in range(loads):
        caption_loads[b].wait()
        part = pl.ds(b * CHUNK, CHUNK)
        score[:, part] = lax.dot_general(
            images[...], captions[part, :], (((1,), (1,)), ((), ())),
            preferred_element_type=jnp.float32,
        ) * jnp.float32(LOG2E / ENTROPIC)
        for g in range(here // GROUP):
            rows = pl.ds(g * GROUP, GROUP)
            logits = [
                score[rows, pl.ds(b * CHUNK + i * LANES, LANES)] for i in range(CHUNK // LANES)
            ]
            top = tree(jnp.maximum, logits)
            if b:
                old = stat_max[rows, :]
                top = jnp.maximum(top, old)
            total = tree(jnp.add, [jnp.exp2(v - top) for v in logits])
            if b:
                total = total + stat_sum[rows, :] * jnp.exp2(old - top)
            stat_max[rows, :] = top
            stat_sum[rows, :] = total

    log_a = jnp.float32(-math.log2(here * rows_n))
    log_b = jnp.float32(-math.log2(score.shape[1] * cols_n))

    def logit_rows(g):
        rows = pl.ds(g * GROUP, GROUP)
        return rows, [
            score[rows, pl.ds(b * LANES, LANES)] + dual[pl.ds(b, 1), :] for b in range(blocks)
        ]

    def send_image(step):
        for k, p in enumerate(col_peers):
            send(
                image_src.at[step], image_recv.at[step, k],
                image_ssem.at[step], image_rsem.at[step], col_peer(*p),
            )

    def get_image(step):
        drain(image_recv.at[step], image_rsem.at[step])
        return lse_of(
            [image_src[step]] + [image_recv[step, k] for k in range(len(col_peers))]
        )

    def send_caption(step, slot, device):
        send(
            caption_src.at[step], caption_recv.at[step, slot],
            caption_ssem.at[step], caption_rsem.at[step], device,
        )

    for step in range(ITERS):
        for g in range(here // GROUP if step else 0):
            rows, logits = logit_rows(g)
            top = tree(jnp.maximum, logits)
            stat_max[rows, :] = top
            stat_sum[rows, :] = tree(jnp.add, [jnp.exp2(v - top) for v in logits])
        lane_max = stat_max[...].T
        top = jnp.max(lane_max, axis=0, keepdims=True)
        total = jnp.sum(stat_sum[...].T * jnp.exp2(lane_max - top), axis=0, keepdims=True)
        image_src[step] = top + jnp.log2(total)
        if step == 0:
            pl.semaphore_wait(barrier, len(row_peers) + len(col_peers))
        send_image(step)
        image_dual = log_a - get_image(step)
        if step == ITERS - 1:
            image_out[...] = image_dual * jnp.float32(ENTROPIC / LOG2E)
        column = jnp.broadcast_to(image_dual, (LANES, here)).T
        for b in range(blocks):
            logits = score[:, pl.ds(b * LANES, LANES)] + column
            top = jnp.max(logits, axis=0, keepdims=True)
            block_max[pl.ds(b, 1), :] = top
            block_sum[pl.ds(b, 1), :] = jnp.sum(jnp.exp2(logits - top), axis=0, keepdims=True)
        caption_src[step] = block_max[...] + jnp.log2(block_sum[...])
        if step < ITERS - 1:
            for k, p in enumerate(row_peers):
                send_caption(step, k, row_peer(*p))
        else:
            for zt in range(z_n):
                dz = lax.rem(zt - z + z_n, z_n)
                for dx in sorted(range(1, x_n), key=lambda p: -ring(p, x_n)):
                    send_caption(step, dz * x_n + dx - 1, row_peer(dz, dx))

                @pl.when(dz != 0)
                def _():
                    send_caption(step, dz * x_n - 1, row_peer(dz, 0))

        drain(caption_recv.at[step], caption_rsem.at[step])
        dual[...] = log_b - lse_of(
            [caption_src[step]] + [caption_recv[step, k] for k in range(len(row_peers))]
        )

    caption_out[...] = dual[...] * jnp.float32(ENTROPIC / LOG2E)
    for g in range(here // GROUP):
        rows, logits = logit_rows(g)
        top = jnp.max(tree(jnp.maximum, logits), axis=1, keepdims=True)
        stat_max[rows, :] = jnp.broadcast_to(top, (GROUP, LANES))
        terms = [jnp.exp2(v - top) for v in logits]
        stat_sum[rows, :] = tree(jnp.add, terms)
        for b, w in enumerate(terms):
            weights[rows, pl.ds(b * LANES, LANES)] = w.astype(jnp.bfloat16)
    def chunk(yt, of_core):
        return pl.ds(pl.multiple_of((2 * yt + of_core) * share, 8), share)

    made = set()
    for q, yt in enumerate(y_order):
        for b in range(2 * share * yt // LANES, -(-2 * share * (yt + 1) // LANES)):
            if b not in made:
                made.add(b)
                part = pl.ds(b * LANES, LANES)
                numer[part, :] = jnp.dot(
                    weights[...], captions[:, part], preferred_element_type=jnp.float32
                ).T
        send(
            numer.at[chunk(yt, 1 - core)], pair_recv.at[yt],
            pair_ssem, pair_rsem.at[yt], col_peer(0, 1),
        )
        if q == 0:
            own = tail_recv.at[c]
            own[0:1, :] = stat_max[...].T[0:1, :]
            own[1:2, :] = jnp.sum(stat_sum[...].T, axis=0, keepdims=True)
            tail_src[...] = own[...]
            for k, p in enumerate(col_peers):
                send(tail_src, tail_recv.at[c], tail_ssem, tail_rsem.at[min(k, 1)], col_peer(*p))

    other = tail_recv.at[c + 1 - 2 * core]
    drain(other, tail_rsem.at[0])
    pair_top = jnp.maximum(tail_src[0:1, :], other[0:1, :])
    own_scale = jnp.exp2(tail_src[0:1, :] - pair_top)
    other_scale = jnp.exp2(other[0:1, :] - pair_top)
    for yt in y_order:
        drain(pair_recv.at[yt], pair_rsem.at[yt])
        y_src[yt] = numer[chunk(yt, core), :] * own_scale + pair_recv[yt] * other_scale

        @pl.when(yt != y)
        def _():
            send(y_src.at[yt], y_recv.at[y], y_ssem, y_rsem, (r, 2 * yt + core))

    y_recv[y] = y_src[y]
    drain(tail_recv.at[pl.ds(0, cols_n - 2)], tail_rsem.at[1])
    tops = [tail_recv[k, 0:1, :] for k in range(cols_n)]
    top = tree(jnp.maximum, tops)
    mass = tree(jnp.add, [tail_recv[k, 1:2, :] * jnp.exp2(tops[k] - top) for k in range(cols_n)])
    inverse = 1.0 / mass
    factor = [
        jnp.exp2(jnp.maximum(tops[2 * k], tops[2 * k + 1]) - top) * inverse for k in range(y_n)
    ]
    drain(y_recv.at[pl.ds(0, y_n - 1)], y_rsem)
    mapped_out[...] = tree(jnp.add, [y_recv[k] * factor[k] for k in range(y_n)])

    drain(tail_recv.at[pl.ds(0, cols_n - 1)], tail_ssem)
    drain(pair_recv, pair_ssem)
    drain(y_recv.at[pl.ds(0, y_n - 1)], y_ssem)
    for step in range(ITERS):
        drain(image_recv.at[step], image_ssem.at[step])
        drain(caption_recv.at[step], caption_ssem.at[step])


def place(image_dual, caption_dual, mapped, image_out, caption_out, mapped_out, sems):
    pairs = ((mapped, mapped_out), (caption_dual, caption_out), (image_dual, image_out))
    copies = [pltpu.make_async_copy(a, b, sems.at[i]) for i, (a, b) in enumerate(pairs)]
    for copy in copies:
        copy.start()
    for copy in copies:
        copy.wait()


def solution(mesh):
    rows_n, cols_n = mesh.shape["row"], mesh.shape["col"]
    y_n = cols_n // 2

    def per_device(images, captions):
        here, width = images.shape
        cols = captions.shape[0]
        share = width // cols_n
        blocks = cols // LANES
        f32 = jnp.float32
        vmem = pl.BlockSpec(memory_space=pltpu.VMEM)
        dma = pltpu.SemaphoreType.DMA
        shapes = ((1, here), (blocks, LANES), (share, here))
        parts = pl.pallas_call(
            functools.partial(kernel, rows_n, cols_n),
            out_shape=tuple(pltpu.VMEM(shape, f32) for shape in shapes),
            in_specs=[pl.BlockSpec(memory_space=pl.ANY)] * 2,
            out_specs=(vmem, vmem, vmem),
            scratch_shapes=[
                pltpu.VMEM((here, width), jnp.bfloat16),
                pltpu.VMEM((cols, width), jnp.bfloat16),
                pltpu.VMEM((here, cols), f32),
                pltpu.VMEM((here, cols), jnp.bfloat16),
                pltpu.VMEM((here, LANES), f32),
                pltpu.VMEM((here, LANES), f32),
                pltpu.VMEM((blocks, LANES), f32),
                pltpu.VMEM((blocks, LANES), f32),
                pltpu.VMEM((blocks, LANES), f32),
                pltpu.VMEM((ITERS, 1, here), f32),
                pltpu.VMEM((ITERS, cols_n - 1, 1, here), f32),
                pltpu.VMEM((ITERS, blocks, LANES), f32),
                pltpu.VMEM((ITERS, rows_n - 1, blocks, LANES), f32),
                pltpu.VMEM((2, here), f32),
                pltpu.VMEM((cols_n, 2, here), f32),
                pltpu.VMEM((width, here), f32),
                pltpu.VMEM((y_n, share, here), f32),
                pltpu.VMEM((y_n, share, here), f32),
                pltpu.VMEM((y_n, share, here), f32),
                dma((cols // CHUNK + 1,)),
                dma((ITERS,)),
                dma((ITERS,)),
                dma((ITERS,)),
                dma((ITERS,)),
                dma,
                dma((2,)),
                dma,
                dma((y_n,)),
                dma,
                dma,
            ],
            compiler_params=pltpu.CompilerParams(
                collective_id=0, has_side_effects=True, vmem_limit_bytes=60 * 2**20
            ),
            name="sinkhorn",
        )(images, captions)
        image_dual, caption_dual, mapped = pl.pallas_call(
            place,
            out_shape=tuple(jax.ShapeDtypeStruct(shape, f32) for shape in shapes),
            in_specs=[vmem] * 3,
            out_specs=[pl.BlockSpec(memory_space=pl.ANY)] * 3,
            scratch_shapes=[dma((3,))],
            name="place",
        )(*[pltpu.with_memory_space_constraint(p, pltpu.VMEM) for p in parts])
        return image_dual.reshape(here), caption_dual.reshape(cols), mapped.T

    return jax.shard_map(
        per_device,
        mesh=mesh,
        in_specs=(P("row", None), P("col", None)),
        out_specs=(P("row"), P("col"), P("row", "col")),
        check_vma=False,
    )
```

```python
import functools
import math

import jax
import jax.numpy as jnp
from jax import lax
from jax.experimental import pallas as pl
from jax.experimental.pallas import tpu as pltpu
from jax.sharding import PartitionSpec as P

MESH = pl.DeviceIdType.MESH
ENTROPIC = 0.05
LOG2E = math.log2(math.e)
ITERS = 2
LANES = 128
GROUP = 16
CHUNK = 512
X_CHIPS = 4
KIND = ('xz', 'xz')
ZORDER = ('far', 'abs')


def ring(offset, size):
    return min(offset, size - offset)


def tree(op, values):
    values = list(values)
    while len(values) > 1:
        rest = [op(a, b) for a, b in zip(values[::2], values[1::2])]
        values = rest + ([values[-1]] if len(values) % 2 else [])
    return values[0]


def lse_of(parts):
    top = tree(jnp.maximum, parts)
    return top + jnp.log2(tree(jnp.add, [jnp.exp2(p - top) for p in parts]))


def send(src, dst, ssem, rsem, device):
    pltpu.make_async_remote_copy(
        src_ref=src, dst_ref=dst, send_sem=ssem, recv_sem=rsem,
        device_id=device, device_id_type=MESH,
    ).start()


def drain(ref, sem):
    pltpu.make_async_copy(ref, ref, sem).wait()


def greet(barrier, device):
    pl.semaphore_signal(barrier, inc=1, device_id=device, device_id_type=MESH)


def kernel(
    rows_n, cols_n, images_hbm, captions_hbm, image_out, caption_out, mapped_out,
    images, captions, score, weights, stat_max, stat_sum, block_max, block_sum, dual,
    image_src, image_recv, caption_src, caption_recv, plane_src, plane_recv, tail_src, tail_recv, numer, pair_recv, y_src, y_recv,
    load_sem, image_ssem, image_rsem, caption_ssem, caption_rsem, plane_ssem, plane_rsem, tail_ssem, tail_rsem,
    pair_ssem, pair_rsem, y_ssem, y_rsem,
):
    here, width = images.shape
    blocks = score.shape[1] // LANES
    loads = captions.shape[0] // CHUNK
    x_n = X_CHIPS
    z_n = rows_n // x_n
    y_n = cols_n // 2
    share = width // cols_n
    r, c = lax.axis_index("row"), lax.axis_index("col")
    z, x, y, core = r // x_n, lax.rem(r, x_n), c // 2, lax.rem(c, 2)

    def row_peer(dz, dx):
        return (lax.rem(z + dz, z_n) * x_n + lax.rem(x + dx, x_n), c)

    def col_peer(dy, dc):
        return (r, lax.rem(y + dy, y_n) * 2 + lax.rem(core + dc, 2))

    x_peers = sorted(range(1, x_n), key=lambda p: -ring(p, x_n))
    z_peers = sorted(range(1, z_n), key=lambda p: -ring(p, z_n))
    row_peers = sorted(
        [(dz, dx) for dz in range(z_n) for dx in range(x_n) if dz or dx],
        key=lambda p: -ring(p[0], z_n) - ring(p[1], x_n),
    )
    col_peers = sorted(
        [(dy, dc) for dy in range(y_n) for dc in range(2) if dy or dc],
        key=lambda p: (p[0] > 0, -ring(p[0], y_n), p[1]),
    )
    y_order = [0, 1, 2, 3, 4, 5, 6, 7]

    image_load = pltpu.make_async_copy(images_hbm, images, load_sem.at[loads])
    image_load.start()
    caption_loads = []
    for b in range(loads):
        part = pl.ds(b * CHUNK, CHUNK)
        caption_loads.append(
            pltpu.make_async_copy(captions_hbm.at[part], captions.at[part], load_sem.at[b])
        )
        caption_loads[-1].start()

    barrier = pltpu.get_barrier_semaphore()
    for p in row_peers:
        greet(barrier, row_peer(*p))
    for p in col_peers:
        greet(barrier, col_peer(*p))

    image_load.wait()
    for b in range(loads):
        caption_loads[b].wait()
        part = pl.ds(b * CHUNK, CHUNK)
        score[:, part] = lax.dot_general(
            images[...], captions[part, :], (((1,), (1,)), ((), ())),
            preferred_element_type=jnp.float32,
        ) * jnp.float32(LOG2E / ENTROPIC)
        for g in range(here // GROUP):
            rows = pl.ds(g * GROUP, GROUP)
            logits = [
                score[rows, pl.ds(b * CHUNK + i * LANES, LANES)] for i in range(CHUNK // LANES)
            ]
            top = tree(jnp.maximum, logits)
            if b:
                old = stat_max[rows, :]
                top = jnp.maximum(top, old)
            total = tree(jnp.add, [jnp.exp2(v - top) for v in logits])
            if b:
                total = total + stat_sum[rows, :] * jnp.exp2(old - top)
            stat_max[rows, :] = top
            stat_sum[rows, :] = total

    log_a = jnp.float32(-math.log2(here * rows_n))
    log_b = jnp.float32(-math.log2(score.shape[1] * cols_n))

    def logit_rows(g):
        rows = pl.ds(g * GROUP, GROUP)
        return rows, [
            score[rows, pl.ds(b * LANES, LANES)] + dual[pl.ds(b, 1), :] for b in range(blocks)
        ]

    def send_image(step):
        for k, p in enumerate(col_peers):
            send(
                image_src.at[step], image_recv.at[step, k],
                image_ssem.at[step], image_rsem.at[step], col_peer(*p),
            )

    def get_image(step):
        drain(image_recv.at[step], image_rsem.at[step])
        return lse_of(
            [image_src[step]] + [image_recv[step, k] for k in range(len(col_peers))]
        )

    def send_caption(step, slot, device):
        send(
            caption_src.at[step], caption_recv.at[step, slot],
            caption_ssem.at[step], caption_rsem.at[step], device,
        )

    def send_plane(step, slot, device):
        send(
            plane_src.at[step], plane_recv.at[step, slot],
            plane_ssem.at[step], plane_rsem.at[step], device,
        )

    def to_z(step, put, slot_of):
        if ZORDER[step] == "far":
            for dz in z_peers:
                put(step, slot_of(dz), row_peer(dz, 0))
        else:
            for zt in range(z_n):
                dz = lax.rem(zt - z + z_n, z_n)

                @pl.when(dz != 0)
                def _():
                    put(step, slot_of(dz), row_peer(dz, 0))

    def to_x(step, put):
        for dx in x_peers:
            put(step, dx - 1, row_peer(0, dx))

    def exchange_caption(step):
        own = caption_src[step]
        if KIND[step] == "direct":
            for zt in range(z_n):
                dz = lax.rem(zt - z + z_n, z_n)
                for dx in x_peers:
                    send_caption(step, dz * x_n + dx - 1, row_peer(dz, dx))

                @pl.when(dz != 0)
                def _():
                    send_caption(step, dz * x_n - 1, row_peer(dz, 0))

            drain(caption_recv.at[step], caption_rsem.at[step])
            return lse_of([own] + [caption_recv[step, k] for k in range(len(row_peers))])
        n, m = (x_n - 1, z_n - 1) if KIND[step] == "xz" else (z_n - 1, x_n - 1)
        if KIND[step] == "xz":
            to_x(step, send_caption)
        else:
            to_z(step, send_caption, lambda dz: dz - 1)
        drain(caption_recv.at[step, pl.ds(0, n)], caption_rsem.at[step])
        plane = lse_of([own] + [caption_recv[step, k] for k in range(n)])
        plane_src[step] = plane
        if KIND[step] == "xz":
            to_z(step, send_plane, lambda dz: dz - 1)
        else:
            to_x(step, send_plane)
        drain(plane_recv.at[step, pl.ds(0, m)], plane_rsem.at[step])
        return lse_of([plane] + [plane_recv[step, k] for k in range(m)])

    for step in range(ITERS):
        for g in range(here // GROUP if step else 0):
            rows, logits = logit_rows(g)
            top = tree(jnp.maximum, logits)
            stat_max[rows, :] = top
            stat_sum[rows, :] = tree(jnp.add, [jnp.exp2(v - top) for v in logits])
        lane_max = stat_max[...].T
        top = jnp.max(lane_max, axis=0, keepdims=True)
        total = jnp.sum(stat_sum[...].T * jnp.exp2(lane_max - top), axis=0, keepdims=True)
        image_src[step] = top + jnp.log2(total)
        if step == 0:
            pl.semaphore_wait(barrier, len(row_peers) + len(col_peers))
        send_image(step)
        image_dual = log_a - get_image(step)
        if step == ITERS - 1:
            image_out[...] = image_dual * jnp.float32(ENTROPIC / LOG2E)
        column = jnp.broadcast_to(image_dual, (LANES, here)).T
        for b in range(blocks):
            logits = score[:, pl.ds(b * LANES, LANES)] + column
            top = jnp.max(logits, axis=0, keepdims=True)
            block_max[pl.ds(b, 1), :] = top
            block_sum[pl.ds(b, 1), :] = jnp.sum(jnp.exp2(logits - top), axis=0, keepdims=True)
        caption_src[step] = block_max[...] + jnp.log2(block_sum[...])
        dual[...] = log_b - exchange_caption(step)

    caption_out[...] = dual[...] * jnp.float32(ENTROPIC / LOG2E)
    for g in range(here // GROUP):
        rows, logits = logit_rows(g)
        top = jnp.max(tree(jnp.maximum, logits), axis=1, keepdims=True)
        stat_max[rows, :] = jnp.broadcast_to(top, (GROUP, LANES))
        terms = [jnp.exp2(v - top) for v in logits]
        stat_sum[rows, :] = tree(jnp.add, terms)
        for b, w in enumerate(terms):
            weights[rows, pl.ds(b * LANES, LANES)] = w.astype(jnp.bfloat16)
    def chunk(yt, of_core):
        return pl.ds(pl.multiple_of((2 * yt + of_core) * share, 8), share)

    made = set()
    for q, yt in enumerate(y_order):
        for b in range(2 * share * yt // LANES, -(-2 * share * (yt + 1) // LANES)):
            if b not in made:
                made.add(b)
                part = pl.ds(b * LANES, LANES)
                numer[part, :] = jnp.dot(
                    weights[...], captions[:, part], preferred_element_type=jnp.float32
                ).T
        send(
            numer.at[chunk(yt, 1 - core)], pair_recv.at[yt],
            pair_ssem, pair_rsem.at[yt], col_peer(0, 1),
        )
        if q == 0:
            own = tail_recv.at[c]
            own[0:1, :] = stat_max[...].T[0:1, :]
            own[1:2, :] = jnp.sum(stat_sum[...].T, axis=0, keepdims=True)
            tail_src[...] = own[...]
            for k, p in enumerate(col_peers):
                send(tail_src, tail_recv.at[c], tail_ssem, tail_rsem.at[min(k, 1)], col_peer(*p))

    other = tail_recv.at[c + 1 - 2 * core]
    drain(other, tail_rsem.at[0])
    pair_top = jnp.maximum(tail_src[0:1, :], other[0:1, :])
    own_scale = jnp.exp2(tail_src[0:1, :] - pair_top)
    other_scale = jnp.exp2(other[0:1, :] - pair_top)
    for yt in y_order:
        drain(pair_recv.at[yt], pair_rsem.at[yt])
        y_src[yt] = numer[chunk(yt, core), :] * own_scale + pair_recv[yt] * other_scale

        @pl.when(yt != y)
        def _():
            send(y_src.at[yt], y_recv.at[y], y_ssem, y_rsem, (r, 2 * yt + core))

    y_recv[y] = y_src[y]
    drain(tail_recv.at[pl.ds(0, cols_n - 2)], tail_rsem.at[1])
    tops = [tail_recv[k, 0:1, :] for k in range(cols_n)]
    top = tree(jnp.maximum, tops)
    mass = tree(jnp.add, [tail_recv[k, 1:2, :] * jnp.exp2(tops[k] - top) for k in range(cols_n)])
    inverse = 1.0 / mass
    factor = [
        jnp.exp2(jnp.maximum(tops[2 * k], tops[2 * k + 1]) - top) * inverse for k in range(y_n)
    ]
    drain(y_recv.at[pl.ds(0, y_n - 1)], y_rsem)
    mapped_out[...] = tree(jnp.add, [y_recv[k] * factor[k] for k in range(y_n)])

    drain(tail_recv.at[pl.ds(0, cols_n - 1)], tail_ssem)
    drain(pair_recv, pair_ssem)
    drain(y_recv.at[pl.ds(0, y_n - 1)], y_ssem)
    for step in range(ITERS):
        drain(image_recv.at[step], image_ssem.at[step])
        if KIND[step] == "direct":
            drain(caption_recv.at[step], caption_ssem.at[step])
        else:
            n, m = (x_n - 1, z_n - 1) if KIND[step] == "xz" else (z_n - 1, x_n - 1)
            drain(caption_recv.at[step, pl.ds(0, n)], caption_ssem.at[step])
            drain(plane_recv.at[step, pl.ds(0, m)], plane_ssem.at[step])


def place(image_dual, caption_dual, mapped, image_out, caption_out, mapped_out, sems):
    pairs = ((mapped, mapped_out), (caption_dual, caption_out), (image_dual, image_out))
    copies = [pltpu.make_async_copy(a, b, sems.at[i]) for i, (a, b) in enumerate(pairs)]
    for copy in copies:
        copy.start()
    for copy in copies:
        copy.wait()


def solution(mesh):
    rows_n, cols_n = mesh.shape["row"], mesh.shape["col"]
    y_n = cols_n // 2

    def per_device(images, captions):
        here, width = images.shape
        cols = captions.shape[0]
        share = width // cols_n
        blocks = cols // LANES
        f32 = jnp.float32
        vmem = pl.BlockSpec(memory_space=pltpu.VMEM)
        dma = pltpu.SemaphoreType.DMA
        shapes = ((1, here), (blocks, LANES), (share, here))
        parts = pl.pallas_call(
            functools.partial(kernel, rows_n, cols_n),
            out_shape=tuple(pltpu.VMEM(shape, f32) for shape in shapes),
            in_specs=[pl.BlockSpec(memory_space=pl.ANY)] * 2,
            out_specs=(vmem, vmem, vmem),
            scratch_shapes=[
                pltpu.VMEM((here, width), jnp.bfloat16),
                pltpu.VMEM((cols, width), jnp.bfloat16),
                pltpu.VMEM((here, cols), f32),
                pltpu.VMEM((here, cols), jnp.bfloat16),
                pltpu.VMEM((here, LANES), f32),
                pltpu.VMEM((here, LANES), f32),
                pltpu.VMEM((blocks, LANES), f32),
                pltpu.VMEM((blocks, LANES), f32),
                pltpu.VMEM((blocks, LANES), f32),
                pltpu.VMEM((ITERS, 1, here), f32),
                pltpu.VMEM((ITERS, cols_n - 1, 1, here), f32),
                pltpu.VMEM((ITERS, blocks, LANES), f32),
                pltpu.VMEM((ITERS, rows_n - 1, blocks, LANES), f32),
                pltpu.VMEM((ITERS, blocks, LANES), f32),
                pltpu.VMEM((ITERS, rows_n // X_CHIPS + X_CHIPS, blocks, LANES), f32),
                pltpu.VMEM((2, here), f32),
                pltpu.VMEM((cols_n, 2, here), f32),
                pltpu.VMEM((width, here), f32),
                pltpu.VMEM((y_n, share, here), f32),
                pltpu.VMEM((y_n, share, here), f32),
                pltpu.VMEM((y_n, share, here), f32),
                dma((cols // CHUNK + 1,)),
                dma((ITERS,)),
                dma((ITERS,)),
                dma((ITERS,)),
                dma((ITERS,)),
                dma((ITERS,)),
                dma((ITERS,)),
                dma,
                dma((2,)),
                dma,
                dma((y_n,)),
                dma,
                dma,
            ],
            compiler_params=pltpu.CompilerParams(
                collective_id=0, has_side_effects=True, vmem_limit_bytes=60 * 2**20
            ),
            name="sinkhorn",
        )(images, captions)
        image_dual, caption_dual, mapped = pl.pallas_call(
            place,
            out_shape=tuple(jax.ShapeDtypeStruct(shape, f32) for shape in shapes),
            in_specs=[vmem] * 3,
            out_specs=[pl.BlockSpec(memory_space=pl.ANY)] * 3,
            scratch_shapes=[dma((3,))],
            name="place",
        )(*[pltpu.with_memory_space_constraint(p, pltpu.VMEM) for p in parts])
        return image_dual.reshape(here), caption_dual.reshape(cols), mapped.T

    return jax.shard_map(
        per_device,
        mesh=mesh,
        in_specs=(P("row", None), P("col", None)),
        out_specs=(P("row"), P("col"), P("row", "col")),
        check_vma=False,
    )
```

```python
import functools
import math

import jax
import jax.numpy as jnp
from jax import lax
from jax.experimental import pallas as pl
from jax.experimental.pallas import tpu as pltpu
from jax.sharding import PartitionSpec as P

MESH = pl.DeviceIdType.MESH
ENTROPIC = 0.05
LOG2E = math.log2(math.e)
ITERS = 2
LANES = 128
GROUP = 16
CHUNK = 512
X_CHIPS = 4
EARLY = (0,)


def ring(offset, size):
    return min(offset, size - offset)


def tree(op, values):
    values = list(values)
    while len(values) > 1:
        rest = [op(a, b) for a, b in zip(values[::2], values[1::2])]
        values = rest + ([values[-1]] if len(values) % 2 else [])
    return values[0]


def lse_of(parts):
    top = tree(jnp.maximum, parts)
    return top + jnp.log2(tree(jnp.add, [jnp.exp2(p - top) for p in parts]))


def send(src, dst, ssem, rsem, device):
    pltpu.make_async_remote_copy(
        src_ref=src, dst_ref=dst, send_sem=ssem, recv_sem=rsem,
        device_id=device, device_id_type=MESH,
    ).start()


def drain(ref, sem):
    pltpu.make_async_copy(ref, ref, sem).wait()


def greet(barrier, device):
    pl.semaphore_signal(barrier, inc=1, device_id=device, device_id_type=MESH)


def kernel(
    rows_n, cols_n, images_hbm, captions_hbm, image_out, caption_out, mapped_out,
    images, captions, score, weights, stat_max, stat_sum, block_max, block_sum, dual,
    image_src, image_recv, caption_src, x_recv, plane_src, z_recv, early_recv, joined, tail_src, tail_recv, numer, pair_recv, y_src, y_recv,
    load_sem, image_ssem, image_rsem, x_ssem, x_rsem, z_ssem, z_rsem,
    early_ssem, early_rsem, tail_ssem, tail_rsem,
    pair_ssem, pair_rsem, y_ssem, y_rsem,
):
    here, width = images.shape
    blocks = score.shape[1] // LANES
    loads = captions.shape[0] // CHUNK
    x_n = X_CHIPS
    z_n = rows_n // x_n
    y_n = cols_n // 2
    share = width // cols_n
    r, c = lax.axis_index("row"), lax.axis_index("col")
    z, x, y, core = r // x_n, lax.rem(r, x_n), c // 2, lax.rem(c, 2)

    def row_peer(dz, dx):
        return (lax.rem(z + dz, z_n) * x_n + lax.rem(x + dx, x_n), c)

    def col_peer(dy, dc):
        return (r, lax.rem(y + dy, y_n) * 2 + lax.rem(core + dc, 2))

    x_peers = sorted(range(1, x_n), key=lambda p: -ring(p, x_n))
    early = functools.reduce(jnp.logical_or, [z == zt for zt in EARLY])
    col_peers = sorted(
        [(dy, dc) for dy in range(y_n) for dc in range(2) if dy or dc],
        key=lambda p: (p[0] > 0, -ring(p[0], y_n), p[1]),
    )
    y_order = list(range(y_n))

    image_load = pltpu.make_async_copy(images_hbm, images, load_sem.at[loads])
    image_load.start()
    caption_loads = []
    for b in range(loads):
        part = pl.ds(b * CHUNK, CHUNK)
        caption_loads.append(
            pltpu.make_async_copy(captions_hbm.at[part], captions.at[part], load_sem.at[b])
        )
        caption_loads[-1].start()

    barrier = pltpu.get_barrier_semaphore()
    for dz in range(1, z_n):
        greet(barrier, row_peer(dz, 0))
    for dx in x_peers:
        greet(barrier, row_peer(0, dx))

    @pl.when(early)
    def _():
        for dz in range(1, z_n):
            for dx in x_peers:
                greet(barrier, row_peer(dz, dx))

    for p in col_peers:
        greet(barrier, col_peer(*p))

    image_load.wait()
    for b in range(loads):
        caption_loads[b].wait()
        part = pl.ds(b * CHUNK, CHUNK)
        score[:, part] = lax.dot_general(
            images[...], captions[part, :], (((1,), (1,)), ((), ())),
            preferred_element_type=jnp.float32,
        ) * jnp.float32(LOG2E / ENTROPIC)
        for g in range(here // GROUP):
            rows = pl.ds(g * GROUP, GROUP)
            logits = [
                score[rows, pl.ds(b * CHUNK + i * LANES, LANES)] for i in range(CHUNK // LANES)
            ]
            top = tree(jnp.maximum, logits)
            if b:
                old = stat_max[rows, :]
                top = jnp.maximum(top, old)
            total = tree(jnp.add, [jnp.exp2(v - top) for v in logits])
            if b:
                total = total + stat_sum[rows, :] * jnp.exp2(old - top)
            stat_max[rows, :] = top
            stat_sum[rows, :] = total

    log_a = jnp.float32(-math.log2(here * rows_n))
    log_b = jnp.float32(-math.log2(score.shape[1] * cols_n))

    def logit_rows(g):
        rows = pl.ds(g * GROUP, GROUP)
        return rows, [
            score[rows, pl.ds(b * LANES, LANES)] + dual[pl.ds(b, 1), :] for b in range(blocks)
        ]

    def send_image(step):
        for k, p in enumerate(col_peers):
            send(
                image_src.at[step], image_recv.at[step, k],
                image_ssem.at[step], image_rsem.at[step], col_peer(*p),
            )

    def get_image(step):
        drain(image_recv.at[step], image_rsem.at[step])
        return lse_of(
            [image_src[step]] + [image_recv[step, k] for k in range(len(col_peers))]
        )

    def exchange_caption(step):
        last = step == ITERS - 1
        if last:
            for zt in EARLY:
                dz = lax.rem(zt - z + z_n, z_n)

                @pl.when(dz != 0)
                def _():
                    for dx in x_peers + [0]:
                        send(
                            caption_src.at[step], early_recv.at[(dz - 1) * x_n + dx],
                            early_ssem, early_rsem, row_peer(dz, dx),
                        )

        for dx in x_peers:
            send(
                caption_src.at[step], x_recv.at[step, dx - 1],
                x_ssem.at[step], x_rsem.at[step], row_peer(0, dx),
            )
        drain(x_recv.at[step], x_rsem.at[step])
        plane = lse_of([caption_src[step]] + [x_recv[step, k] for k in range(x_n - 1)])
        plane_src[step] = plane
        for zt in range(z_n):
            if last and zt in EARLY:
                continue
            dz = lax.rem(zt - z + z_n, z_n)

            @pl.when(dz != 0)
            def _():
                send(
                    plane_src.at[step], z_recv.at[step, dz - 1],
                    z_ssem.at[step], z_rsem.at[step], row_peer(dz, 0),
                )

        if not last:
            drain(z_recv.at[step], z_rsem.at[step])
            return lse_of([plane] + [z_recv[step, k] for k in range(z_n - 1)])

        @pl.when(jnp.logical_not(early))
        def _():
            drain(z_recv.at[step], z_rsem.at[step])
            joined[...] = lse_of([plane] + [z_recv[step, k] for k in range(z_n - 1)])

        @pl.when(early)
        def _():
            drain(early_recv, early_rsem)
            joined[...] = lse_of([plane] + [early_recv[k] for k in range(early_recv.shape[0])])

        return joined[...]

    for step in range(ITERS):
        for g in range(here // GROUP if step else 0):
            rows, logits = logit_rows(g)
            top = tree(jnp.maximum, logits)
            stat_max[rows, :] = top
            stat_sum[rows, :] = tree(jnp.add, [jnp.exp2(v - top) for v in logits])
        lane_max = stat_max[...].T
        top = jnp.max(lane_max, axis=0, keepdims=True)
        total = jnp.sum(stat_sum[...].T * jnp.exp2(lane_max - top), axis=0, keepdims=True)
        image_src[step] = top + jnp.log2(total)
        if step == 0:
            near = z_n + x_n - 2 + len(col_peers)
            others = (x_n - 1) * (len(EARLY) - early.astype(jnp.int32))
            pl.semaphore_wait(barrier, near + others)
        send_image(step)
        image_dual = log_a - get_image(step)
        if step == ITERS - 1:
            image_out[...] = image_dual * jnp.float32(ENTROPIC / LOG2E)
        column = jnp.broadcast_to(image_dual, (LANES, here)).T
        for b in range(blocks):
            logits = score[:, pl.ds(b * LANES, LANES)] + column
            top = jnp.max(logits, axis=0, keepdims=True)
            block_max[pl.ds(b, 1), :] = top
            block_sum[pl.ds(b, 1), :] = jnp.sum(jnp.exp2(logits - top), axis=0, keepdims=True)
        caption_src[step] = block_max[...] + jnp.log2(block_sum[...])
        dual[...] = log_b - exchange_caption(step)

    caption_out[...] = dual[...] * jnp.float32(ENTROPIC / LOG2E)
    for g in range(here // GROUP):
        rows, logits = logit_rows(g)
        top = jnp.max(tree(jnp.maximum, logits), axis=1, keepdims=True)
        stat_max[rows, :] = jnp.broadcast_to(top, (GROUP, LANES))
        terms = [jnp.exp2(v - top) for v in logits]
        stat_sum[rows, :] = tree(jnp.add, terms)
        for b, w in enumerate(terms):
            weights[rows, pl.ds(b * LANES, LANES)] = w.astype(jnp.bfloat16)
    def chunk(yt, of_core):
        return pl.ds(pl.multiple_of((2 * yt + of_core) * share, 8), share)

    made = set()
    for q, yt in enumerate(y_order):
        for b in range(2 * share * yt // LANES, -(-2 * share * (yt + 1) // LANES)):
            if b not in made:
                made.add(b)
                part = pl.ds(b * LANES, LANES)
                numer[part, :] = jnp.dot(
                    weights[...], captions[:, part], preferred_element_type=jnp.float32
                ).T
        send(
            numer.at[chunk(yt, 1 - core)], pair_recv.at[yt],
            pair_ssem, pair_rsem.at[yt], col_peer(0, 1),
        )
        if q == 0:
            own = tail_recv.at[c]
            own[0:1, :] = stat_max[...].T[0:1, :]
            own[1:2, :] = jnp.sum(stat_sum[...].T, axis=0, keepdims=True)
            tail_src[...] = own[...]
            for k, p in enumerate(col_peers):
                send(tail_src, tail_recv.at[c], tail_ssem, tail_rsem.at[min(k, 1)], col_peer(*p))

    other = tail_recv.at[c + 1 - 2 * core]
    drain(other, tail_rsem.at[0])
    pair_top = jnp.maximum(tail_src[0:1, :], other[0:1, :])
    own_scale = jnp.exp2(tail_src[0:1, :] - pair_top)
    other_scale = jnp.exp2(other[0:1, :] - pair_top)
    for yt in y_order:
        drain(pair_recv.at[yt], pair_rsem.at[yt])
        y_src[yt] = numer[chunk(yt, core), :] * own_scale + pair_recv[yt] * other_scale

        @pl.when(yt != y)
        def _():
            send(y_src.at[yt], y_recv.at[y], y_ssem, y_rsem, (r, 2 * yt + core))

    y_recv[y] = y_src[y]
    drain(tail_recv.at[pl.ds(0, cols_n - 2)], tail_rsem.at[1])
    tops = [tail_recv[k, 0:1, :] for k in range(cols_n)]
    top = tree(jnp.maximum, tops)
    mass = tree(jnp.add, [tail_recv[k, 1:2, :] * jnp.exp2(tops[k] - top) for k in range(cols_n)])
    inverse = 1.0 / mass
    factor = [
        jnp.exp2(jnp.maximum(tops[2 * k], tops[2 * k + 1]) - top) * inverse for k in range(y_n)
    ]
    drain(y_recv.at[pl.ds(0, y_n - 1)], y_rsem)
    mapped_out[...] = tree(jnp.add, [y_recv[k] * factor[k] for k in range(y_n)])

    drain(tail_recv.at[pl.ds(0, cols_n - 1)], tail_ssem)
    drain(pair_recv, pair_ssem)
    drain(y_recv.at[pl.ds(0, y_n - 1)], y_ssem)
    for step in range(ITERS):
        drain(image_recv.at[step], image_ssem.at[step])
        drain(x_recv.at[step], x_ssem.at[step])
    for step in range(ITERS - 1):
        drain(z_recv.at[step], z_ssem.at[step])

    @pl.when(early)
    def _():
        drain(z_recv.at[ITERS - 1, pl.ds(0, z_n - len(EARLY))], z_ssem.at[ITERS - 1])
        if len(EARLY) > 1:
            drain(early_recv.at[pl.ds(0, (len(EARLY) - 1) * x_n)], early_ssem)

    @pl.when(jnp.logical_not(early))
    def _():
        drain(z_recv.at[ITERS - 1, pl.ds(0, z_n - 1 - len(EARLY))], z_ssem.at[ITERS - 1])
        drain(early_recv.at[pl.ds(0, len(EARLY) * x_n)], early_ssem)


def place(image_dual, caption_dual, mapped, image_out, caption_out, mapped_out, sems):
    pairs = ((mapped, mapped_out), (caption_dual, caption_out), (image_dual, image_out))
    copies = [pltpu.make_async_copy(a, b, sems.at[i]) for i, (a, b) in enumerate(pairs)]
    for copy in copies:
        copy.start()
    for copy in copies:
        copy.wait()


def solution(mesh):
    rows_n, cols_n = mesh.shape["row"], mesh.shape["col"]
    y_n = cols_n // 2

    def per_device(images, captions):
        here, width = images.shape
        cols = captions.shape[0]
        share = width // cols_n
        blocks = cols // LANES
        f32 = jnp.float32
        vmem = pl.BlockSpec(memory_space=pltpu.VMEM)
        dma = pltpu.SemaphoreType.DMA
        shapes = ((1, here), (blocks, LANES), (share, here))
        parts = pl.pallas_call(
            functools.partial(kernel, rows_n, cols_n),
            out_shape=tuple(pltpu.VMEM(shape, f32) for shape in shapes),
            in_specs=[pl.BlockSpec(memory_space=pl.ANY)] * 2,
            out_specs=(vmem, vmem, vmem),
            scratch_shapes=[
                pltpu.VMEM((here, width), jnp.bfloat16),
                pltpu.VMEM((cols, width), jnp.bfloat16),
                pltpu.VMEM((here, cols), f32),
                pltpu.VMEM((here, cols), jnp.bfloat16),
                pltpu.VMEM((here, LANES), f32),
                pltpu.VMEM((here, LANES), f32),
                pltpu.VMEM((blocks, LANES), f32),
                pltpu.VMEM((blocks, LANES), f32),
                pltpu.VMEM((blocks, LANES), f32),
                pltpu.VMEM((ITERS, 1, here), f32),
                pltpu.VMEM((ITERS, cols_n - 1, 1, here), f32),
                pltpu.VMEM((ITERS, blocks, LANES), f32),
                pltpu.VMEM((ITERS, X_CHIPS - 1, blocks, LANES), f32),
                pltpu.VMEM((ITERS, blocks, LANES), f32),
                pltpu.VMEM((ITERS, rows_n // X_CHIPS - 1, blocks, LANES), f32),
                pltpu.VMEM((rows_n - X_CHIPS, blocks, LANES), f32),
                pltpu.VMEM((blocks, LANES), f32),
                pltpu.VMEM((2, here), f32),
                pltpu.VMEM((cols_n, 2, here), f32),
                pltpu.VMEM((width, here), f32),
                pltpu.VMEM((y_n, share, here), f32),
                pltpu.VMEM((y_n, share, here), f32),
                pltpu.VMEM((y_n, share, here), f32),
                dma((cols // CHUNK + 1,)),
                dma((ITERS,)),
                dma((ITERS,)),
                dma((ITERS,)),
                dma((ITERS,)),
                dma((ITERS,)),
                dma((ITERS,)),
                dma,
                dma,
                dma,
                dma((2,)),
                dma,
                dma((y_n,)),
                dma,
                dma,
            ],
            compiler_params=pltpu.CompilerParams(
                collective_id=0, has_side_effects=True, vmem_limit_bytes=60 * 2**20
            ),
            name="sinkhorn",
        )(images, captions)
        image_dual, caption_dual, mapped = pl.pallas_call(
            place,
            out_shape=tuple(jax.ShapeDtypeStruct(shape, f32) for shape in shapes),
            in_specs=[vmem] * 3,
            out_specs=[pl.BlockSpec(memory_space=pl.ANY)] * 3,
            scratch_shapes=[dma((3,))],
            name="place",
        )(*[pltpu.with_memory_space_constraint(p, pltpu.VMEM) for p in parts])
        return image_dual.reshape(here), caption_dual.reshape(cols), mapped.T

    return jax.shard_map(
        per_device,
        mesh=mesh,
        in_specs=(P("row", None), P("col", None)),
        out_specs=(P("row"), P("col"), P("row", "col")),
        check_vma=False,
    )
```

```python
import functools
import math

import jax
import jax.numpy as jnp
from jax import lax
from jax.experimental import pallas as pl
from jax.experimental.pallas import tpu as pltpu
from jax.sharding import PartitionSpec as P

MESH = pl.DeviceIdType.MESH
ENTROPIC = 0.05
LOG2E = math.log2(math.e)
ITERS = 2
LANES = 128
GROUP = 16
CHUNK = 512
X_CHIPS = 4


def ring(offset, size):
    return min(offset, size - offset)


def tree(op, values):
    values = list(values)
    while len(values) > 1:
        rest = [op(a, b) for a, b in zip(values[::2], values[1::2])]
        values = rest + ([values[-1]] if len(values) % 2 else [])
    return values[0]


def lse_of(parts):
    top = tree(jnp.maximum, parts)
    return top + jnp.log2(tree(jnp.add, [jnp.exp2(p - top) for p in parts]))


def send(src, dst, ssem, rsem, device):
    pltpu.make_async_remote_copy(
        src_ref=src, dst_ref=dst, send_sem=ssem, recv_sem=rsem,
        device_id=device, device_id_type=MESH,
    ).start()


def drain(ref, sem):
    pltpu.make_async_copy(ref, ref, sem).wait()


def greet(barrier, device):
    pl.semaphore_signal(barrier, inc=1, device_id=device, device_id_type=MESH)


def kernel(
    rows_n, cols_n, images_hbm, captions_hbm, image_out, caption_out, mapped_out,
    images, captions, score, weights, stat_max, stat_sum, block_max, block_sum, dual,
    image_src, image_recv, caption_src, x_recv, cross_recv, plane_src, cross_src, z_recv, first_recv,
    tail_src, tail_recv, numer, pair_recv, y_src, y_recv,
    load_sem, image_ssem, image_rsem, x_ssem, x_rsem, cross_rsem, z_ssem, z_rsem,
    first_ssem, first_rsem, tail_ssem, tail_rsem,
    pair_ssem, pair_rsem, y_ssem, y_rsem,
):
    here, width = images.shape
    blocks = score.shape[1] // LANES
    loads = captions.shape[0] // CHUNK
    x_n = X_CHIPS
    z_n = rows_n // x_n
    y_n = cols_n // 2
    share = width // cols_n
    r, c = lax.axis_index("row"), lax.axis_index("col")
    z, x, y, core = r // x_n, lax.rem(r, x_n), c // 2, lax.rem(c, 2)

    def row_peer(dz, dx):
        return (lax.rem(z + dz, z_n) * x_n + lax.rem(x + dx, x_n), c)

    def cross_peer(dz, dx):
        return (row_peer(dz, dx)[0], c + 1 - 2 * core)

    def col_peer(dy, dc):
        return (r, lax.rem(y + dy, y_n) * 2 + lax.rem(core + dc, 2))

    x_peers = sorted(range(1, x_n), key=lambda p: -ring(p, x_n))
    col_peers = sorted(
        [(dy, dc) for dy in range(y_n) for dc in range(2) if dy or dc],
        key=lambda p: (p[0] > 0, -ring(p[0], y_n), p[1]),
    )
    y_order = list(range(y_n))

    image_load = pltpu.make_async_copy(images_hbm, images, load_sem.at[loads])
    image_load.start()
    caption_loads = []
    for b in range(loads):
        part = pl.ds(b * CHUNK, CHUNK)
        caption_loads.append(
            pltpu.make_async_copy(captions_hbm.at[part], captions.at[part], load_sem.at[b])
        )
        caption_loads[-1].start()

    barrier = pltpu.get_barrier_semaphore()
    z_peers = sorted(range(1, z_n), key=lambda p: -ring(p, z_n))

    @pl.when(core == 0)
    def _():
        for dz in z_peers:
            greet(barrier, cross_peer(dz, 0))

    @pl.when(core != 0)
    def _():
        for dz in z_peers:
            greet(barrier, row_peer(dz, 0))
        for dx in x_peers:
            greet(barrier, row_peer(0, dx))
            greet(barrier, cross_peer(0, dx))

    @pl.when(z == 0)
    def _():
        for dz in z_peers:
            for dx in x_peers:
                greet(barrier, row_peer(dz, dx))

    @pl.when(jnp.logical_and(z == 0, core == 0))
    def _():
        for dz in z_peers:
            greet(barrier, row_peer(dz, 0))

    for p in col_peers:
        greet(barrier, col_peer(*p))

    image_load.wait()
    for b in range(loads):
        caption_loads[b].wait()
        part = pl.ds(b * CHUNK, CHUNK)
        score[:, part] = lax.dot_general(
            images[...], captions[part, :], (((1,), (1,)), ((), ())),
            preferred_element_type=jnp.float32,
        ) * jnp.float32(LOG2E / ENTROPIC)
        for g in range(here // GROUP):
            rows = pl.ds(g * GROUP, GROUP)
            logits = [
                score[rows, pl.ds(b * CHUNK + i * LANES, LANES)] for i in range(CHUNK // LANES)
            ]
            top = tree(jnp.maximum, logits)
            if b:
                old = stat_max[rows, :]
                top = jnp.maximum(top, old)
            total = tree(jnp.add, [jnp.exp2(v - top) for v in logits])
            if b:
                total = total + stat_sum[rows, :] * jnp.exp2(old - top)
            stat_max[rows, :] = top
            stat_sum[rows, :] = total

    log_a = jnp.float32(-math.log2(here * rows_n))
    log_b = jnp.float32(-math.log2(score.shape[1] * cols_n))

    def logit_rows(g):
        rows = pl.ds(g * GROUP, GROUP)
        return rows, [
            score[rows, pl.ds(b * LANES, LANES)] + dual[pl.ds(b, 1), :] for b in range(blocks)
        ]

    def send_image(step):
        for k, p in enumerate(col_peers):
            send(
                image_src.at[step], image_recv.at[step, k],
                image_ssem.at[step], image_rsem.at[step], col_peer(*p),
            )

    def get_image(step):
        drain(image_recv.at[step], image_rsem.at[step])
        return lse_of(
            [image_src[step]] + [image_recv[step, k] for k in range(len(col_peers))]
        )

    def send_first(step):
        dz = lax.rem(z_n - z, z_n)
        for dx in x_peers + [0]:
            send(
                caption_src.at[step], first_recv.at[(dz - 1) * x_n + dx],
                first_ssem, first_rsem, row_peer(dz, dx),
            )

    def send_planes(step, src, of_peer):
        for zt in range(1 if step == ITERS - 1 else 0, z_n):
            dz = lax.rem(zt - z + z_n, z_n)

            @pl.when(dz != 0)
            def _():
                send(
                    src.at[step], z_recv.at[step, dz - 1],
                    z_ssem.at[step], z_rsem.at[step], of_peer(dz, 0),
                )

    def join(step, count, parts):
        drain(z_recv.at[step, pl.ds(0, count)], z_rsem.at[step])
        dual[...] = log_b - lse_of(parts + [z_recv[step, k] for k in range(count)])

    def join_first(parts):
        drain(first_recv, first_rsem)
        dual[...] = log_b - lse_of(parts + [first_recv[k] for k in range(first_recv.shape[0])])

    def exchange_zero(step):
        last = step == ITERS - 1
        if last:
            pl.when(z != 0)(functools.partial(send_first, step))
        for dx in x_peers + [0]:
            send(
                caption_src.at[step], cross_recv.at[step, dx],
                x_ssem.at[step], cross_rsem.at[step], cross_peer(0, dx),
            )

        def normal():
            join(step, z_n, [])

        if not last:
            normal()
            return
        pl.when(z != 0)(normal)

        @pl.when(z == 0)
        def _():
            sibling = z_recv.at[step, z_n - 1]
            drain(sibling, z_rsem.at[step])
            join_first([sibling[...]])

    def exchange_one(step):
        last = step == ITERS - 1
        if last:
            pl.when(z != 0)(functools.partial(send_first, step))
        for dx in x_peers:
            send(
                caption_src.at[step], x_recv.at[step, dx - 1],
                x_ssem.at[step], x_rsem.at[step], row_peer(0, dx),
            )
        drain(x_recv.at[step], x_rsem.at[step])
        plane = lse_of([caption_src[step]] + [x_recv[step, k] for k in range(x_n - 1)])
        plane_src[step] = plane
        send_planes(step, plane_src, row_peer)
        drain(cross_recv.at[step], cross_rsem.at[step])
        cross_src[step] = lse_of([cross_recv[step, k] for k in range(x_n)])
        send_planes(step, cross_src, cross_peer)
        send(
            cross_src.at[step], z_recv.at[step, z_n - 1],
            z_ssem.at[step], z_rsem.at[step], cross_peer(0, 0),
        )

        def normal():
            join(step, z_n - 1, [plane])

        if last:
            pl.when(z != 0)(normal)
            pl.when(z == 0)(functools.partial(join_first, [plane]))
        else:
            normal()

    for step in range(ITERS):
        for g in range(here // GROUP if step else 0):
            rows, logits = logit_rows(g)
            top = tree(jnp.maximum, logits)
            stat_max[rows, :] = top
            stat_sum[rows, :] = tree(jnp.add, [jnp.exp2(v - top) for v in logits])
        lane_max = stat_max[...].T
        top = jnp.max(lane_max, axis=0, keepdims=True)
        total = jnp.sum(stat_sum[...].T * jnp.exp2(lane_max - top), axis=0, keepdims=True)
        image_src[step] = top + jnp.log2(total)
        if step == 0:
            from_zero = x_n - 1 + jnp.where(z == 0, 0, x_n)
            from_one = x_n - 1 + 2 * (z_n - 1) + jnp.where(z == 0, 0, x_n - 1)
            pl.semaphore_wait(barrier, len(col_peers) + jnp.where(core == 0, from_zero, from_one))
        send_image(step)
        image_dual = log_a - get_image(step)
        if step == ITERS - 1:
            image_out[...] = image_dual * jnp.float32(ENTROPIC / LOG2E)
        column = jnp.broadcast_to(image_dual, (LANES, here)).T
        for b in range(blocks):
            block_max[pl.ds(b, 1), :] = jnp.max(
                score[:, pl.ds(b * LANES, LANES)] + column, axis=0, keepdims=True
            )
        for b in range(blocks):
            logits = score[:, pl.ds(b * LANES, LANES)] + column
            block_sum[pl.ds(b, 1), :] = jnp.sum(
                jnp.exp2(logits - block_max[pl.ds(b, 1), :]), axis=0, keepdims=True
            )
        caption_src[step] = block_max[...] + jnp.log2(block_sum[...])
        pl.when(core == 0)(functools.partial(exchange_zero, step))
        pl.when(core != 0)(functools.partial(exchange_one, step))

    caption_out[...] = dual[...] * jnp.float32(ENTROPIC / LOG2E)
    for g in range(here // GROUP):
        rows, logits = logit_rows(g)
        top = jnp.max(tree(jnp.maximum, logits), axis=1, keepdims=True)
        stat_max[rows, :] = jnp.broadcast_to(top, (GROUP, LANES))
        terms = [jnp.exp2(v - top) for v in logits]
        stat_sum[rows, :] = tree(jnp.add, terms)
        for b, w in enumerate(terms):
            weights[rows, pl.ds(b * LANES, LANES)] = w.astype(jnp.bfloat16)
    tail_src[0:1, :] = stat_max[...].T[0:1, :]
    tail_src[1:2, :] = jnp.sum(stat_sum[...].T, axis=0, keepdims=True)

    def chunk(yt, of_core):
        return pl.ds(pl.multiple_of((2 * yt + of_core) * share, 8), share)

    made = set()
    for q, yt in enumerate(y_order):
        for b in range(2 * share * yt // LANES, -(-2 * share * (yt + 1) // LANES)):
            if b not in made:
                made.add(b)
                part = pl.ds(b * LANES, LANES)
                numer[part, :] = jnp.dot(
                    weights[...], captions[:, part], preferred_element_type=jnp.float32
                ).T
        send(
            numer.at[chunk(yt, core)], pair_recv.at[yt],
            pair_ssem, pair_rsem.at[yt], col_peer(0, 1),
        )
        if q == 0:
            tail_recv[c] = tail_src[...]
            for k, p in enumerate(col_peers):
                send(tail_src, tail_recv.at[c], tail_ssem, tail_rsem.at[min(k, 1)], col_peer(*p))

    other = tail_recv.at[c + 1 - 2 * core]
    drain(other, tail_rsem.at[0])
    pair_top = jnp.maximum(tail_src[0:1, :], other[0:1, :])
    own_scale = jnp.exp2(tail_src[0:1, :] - pair_top)
    other_scale = jnp.exp2(other[0:1, :] - pair_top)
    for yt in y_order:
        drain(pair_recv.at[yt], pair_rsem.at[yt])
        y_src[yt] = numer[chunk(yt, 1 - core), :] * own_scale + pair_recv[yt] * other_scale
        send(y_src.at[yt], y_recv.at[y], y_ssem, y_rsem, (r, 2 * yt + 1 - core))

    drain(tail_recv.at[pl.ds(0, cols_n - 2)], tail_rsem.at[1])
    tops = [tail_recv[k, 0:1, :] for k in range(cols_n)]
    top = tree(jnp.maximum, tops)
    mass = tree(jnp.add, [tail_recv[k, 1:2, :] * jnp.exp2(tops[k] - top) for k in range(cols_n)])
    inverse = 1.0 / mass
    factor = [
        jnp.exp2(jnp.maximum(tops[2 * k], tops[2 * k + 1]) - top) * inverse for k in range(y_n)
    ]
    drain(y_recv, y_rsem)
    mapped_out[...] = tree(jnp.add, [y_recv[k] * factor[k] for k in range(y_n)])

    drain(tail_recv.at[pl.ds(0, cols_n - 1)], tail_ssem)
    drain(pair_recv, pair_ssem)
    drain(y_recv, y_ssem)
    for step in range(ITERS):
        drain(image_recv.at[step], image_ssem.at[step])

    @pl.when(z != 0)
    def _():
        drain(first_recv.at[pl.ds(0, x_n)], first_ssem)

    @pl.when(core == 0)
    def _():
        for step in range(ITERS):
            drain(cross_recv.at[step], x_ssem.at[step])

    @pl.when(core != 0)
    def _():
        for step in range(ITERS):
            drain(x_recv.at[step], x_ssem.at[step])
        for step in range(ITERS - 1):
            drain(first_recv.at[pl.ds(0, 2 * z_n - 1)], z_ssem.at[step])

        @pl.when(z == 0)
        def _():
            drain(first_recv.at[pl.ds(0, 2 * z_n - 1)], z_ssem.at[ITERS - 1])

        @pl.when(z != 0)
        def _():
            drain(first_recv.at[pl.ds(0, 2 * z_n - 3)], z_ssem.at[ITERS - 1])


def place(image_dual, caption_dual, mapped, image_out, caption_out, mapped_out, sems):
    pairs = ((mapped, mapped_out), (caption_dual, caption_out), (image_dual, image_out))
    copies = [pltpu.make_async_copy(a, b, sems.at[i]) for i, (a, b) in enumerate(pairs)]
    for copy in copies:
        copy.start()
    for copy in copies:
        copy.wait()


def solution(mesh):
    rows_n, cols_n = mesh.shape["row"], mesh.shape["col"]
    y_n = cols_n // 2

    def per_device(images, captions):
        here, width = images.shape
        cols = captions.shape[0]
        share = width // cols_n
        blocks = cols // LANES
        f32 = jnp.float32
        vmem = pl.BlockSpec(memory_space=pltpu.VMEM)
        dma = pltpu.SemaphoreType.DMA
        shapes = ((1, here), (blocks, LANES), (share, here))
        parts = pl.pallas_call(
            functools.partial(kernel, rows_n, cols_n),
            out_shape=tuple(pltpu.VMEM(shape, f32) for shape in shapes),
            in_specs=[pl.BlockSpec(memory_space=pl.ANY)] * 2,
            out_specs=(vmem, vmem, vmem),
            scratch_shapes=[
                pltpu.VMEM((here, width), jnp.bfloat16),
                pltpu.VMEM((cols, width), jnp.bfloat16),
                pltpu.VMEM((here, cols), f32),
                pltpu.VMEM((here, cols), jnp.bfloat16),
                pltpu.VMEM((here, LANES), f32),
                pltpu.VMEM((here, LANES), f32),
                pltpu.VMEM((blocks, LANES), f32),
                pltpu.VMEM((blocks, LANES), f32),
                pltpu.VMEM((blocks, LANES), f32),
                pltpu.VMEM((ITERS, 1, here), f32),
                pltpu.VMEM((ITERS, cols_n - 1, 1, here), f32),
                pltpu.VMEM((ITERS, blocks, LANES), f32),
                pltpu.VMEM((ITERS, X_CHIPS - 1, blocks, LANES), f32),
                pltpu.VMEM((ITERS, X_CHIPS, blocks, LANES), f32),
                pltpu.VMEM((ITERS, blocks, LANES), f32),
                pltpu.VMEM((ITERS, blocks, LANES), f32),
                pltpu.VMEM((ITERS, rows_n // X_CHIPS, blocks, LANES), f32),
                pltpu.VMEM((rows_n - X_CHIPS, blocks, LANES), f32),
                pltpu.VMEM((2, here), f32),
                pltpu.VMEM((cols_n, 2, here), f32),
                pltpu.VMEM((width, here), f32),
                pltpu.VMEM((y_n, share, here), f32),
                pltpu.VMEM((y_n, share, here), f32),
                pltpu.VMEM((y_n, share, here), f32),
                dma((cols // CHUNK + 1,)),
                dma((ITERS,)),
                dma((ITERS,)),
                dma((ITERS,)),
                dma((ITERS,)),
                dma((ITERS,)),
                dma((ITERS,)),
                dma((ITERS,)),
                dma,
                dma,
                dma,
                dma((2,)),
                dma,
                dma((y_n,)),
                dma,
                dma,
            ],
            compiler_params=pltpu.CompilerParams(
                collective_id=0, has_side_effects=True, vmem_limit_bytes=60 * 2**20
            ),
            name="sinkhorn",
        )(images, captions)
        image_dual, caption_dual, mapped = pl.pallas_call(
            place,
            out_shape=tuple(jax.ShapeDtypeStruct(shape, f32) for shape in shapes),
            in_specs=[vmem] * 3,
            out_specs=[pl.BlockSpec(memory_space=pl.ANY)] * 3,
            scratch_shapes=[dma((3,))],
            name="place",
        )(*[pltpu.with_memory_space_constraint(p, pltpu.VMEM) for p in parts])
        return image_dual.reshape(here), caption_dual.reshape(cols), mapped.T

    return jax.shard_map(
        per_device,
        mesh=mesh,
        in_specs=(P("row", None), P("col", None)),
        out_specs=(P("row"), P("col"), P("row", "col")),
        check_vma=False,
    )
```

```python
import functools
import math

import jax
import jax.numpy as jnp
from jax import lax
from jax.experimental import pallas as pl
from jax.experimental.pallas import tpu as pltpu
from jax.sharding import PartitionSpec as P

MESH = pl.DeviceIdType.MESH
ENTROPIC = 0.05
LOG2E = math.log2(math.e)
ITERS = 2
LANES = 128
GROUP = 16
CHUNK = 512
X_CHIPS = 4


def ring(offset, size):
    return min(offset, size - offset)


def tree(op, values):
    values = list(values)
    while len(values) > 1:
        rest = [op(a, b) for a, b in zip(values[::2], values[1::2])]
        values = rest + ([values[-1]] if len(values) % 2 else [])
    return values[0]


def lse_of(parts):
    top = tree(jnp.maximum, parts)
    return top + jnp.log2(tree(jnp.add, [jnp.exp2(p - top) for p in parts]))


def send(src, dst, ssem, rsem, device):
    pltpu.make_async_remote_copy(
        src_ref=src, dst_ref=dst, send_sem=ssem, recv_sem=rsem,
        device_id=device, device_id_type=MESH,
    ).start()


def drain(ref, sem):
    pltpu.make_async_copy(ref, ref, sem).wait()


def greet(barrier, device):
    pl.semaphore_signal(barrier, inc=1, device_id=device, device_id_type=MESH)


def kernel(
    rows_n, cols_n, images_hbm, captions_hbm, image_out, caption_out, mapped_out,
    images, captions, score, weights, stat_max, stat_sum, block_max, block_sum, dual,
    image_src, image_recv, caption_src, x_recv, cross_recv, plane_src, cross_src, z_recv, first_recv,
    tail_src, tail_recv, numer, pair_recv, y_src, y_recv,
    load_sem, image_ssem, image_rsem, x_ssem, x_rsem, cross_rsem, z_ssem, z_rsem,
    first_ssem, first_rsem, tail_ssem, tail_rsem,
    pair_ssem, pair_rsem, y_ssem, y_rsem,
):
    here, width = images.shape
    blocks = score.shape[1] // LANES
    loads = captions.shape[0] // CHUNK
    x_n = X_CHIPS
    z_n = rows_n // x_n
    y_n = cols_n // 2
    share = width // cols_n
    r, c = lax.axis_index("row"), lax.axis_index("col")
    z, x, y, core = r // x_n, lax.rem(r, x_n), c // 2, lax.rem(c, 2)

    def row_peer(dz, dx):
        return (lax.rem(z + dz, z_n) * x_n + lax.rem(x + dx, x_n), c)

    def cross_peer(dz, dx):
        return (row_peer(dz, dx)[0], c + 1 - 2 * core)

    def col_peer(dy, dc):
        return (r, lax.rem(y + dy, y_n) * 2 + lax.rem(core + dc, 2))

    x_peers = sorted(range(1, x_n), key=lambda p: -ring(p, x_n))
    col_peers = sorted(
        [(dy, dc) for dy in range(y_n) for dc in range(2) if dy or dc],
        key=lambda p: (p[0] > 0, -ring(p[0], y_n), p[1]),
    )
    y_order = list(range(y_n))

    image_load = pltpu.make_async_copy(images_hbm, images, load_sem.at[loads])
    image_load.start()
    caption_loads = []
    for b in range(loads):
        part = pl.ds(b * CHUNK, CHUNK)
        caption_loads.append(
            pltpu.make_async_copy(captions_hbm.at[part], captions.at[part], load_sem.at[b])
        )
        caption_loads[-1].start()

    barrier = pltpu.get_barrier_semaphore()
    z_peers = sorted(range(1, z_n), key=lambda p: -ring(p, z_n))

    @pl.when(core == 0)
    def _():
        for dz in z_peers:
            greet(barrier, cross_peer(dz, 0))

    @pl.when(core != 0)
    def _():
        for dz in z_peers:
            greet(barrier, row_peer(dz, 0))
        for dx in x_peers:
            greet(barrier, row_peer(0, dx))
            greet(barrier, cross_peer(0, dx))

    @pl.when(z == 0)
    def _():
        for dz in z_peers:
            for dx in x_peers:
                greet(barrier, row_peer(dz, dx))

    @pl.when(jnp.logical_and(z == 0, core == 0))
    def _():
        for dz in z_peers:
            greet(barrier, row_peer(dz, 0))

    for p in col_peers:
        greet(barrier, col_peer(*p))

    image_load.wait()
    for b in range(loads):
        caption_loads[b].wait()
        part = pl.ds(b * CHUNK, CHUNK)
        score[:, part] = lax.dot_general(
            images[...], captions[part, :], (((1,), (1,)), ((), ())),
            preferred_element_type=jnp.float32,
        ) * jnp.float32(LOG2E / ENTROPIC)
        for g in range(here // GROUP):
            rows = pl.ds(g * GROUP, GROUP)
            logits = [
                score[rows, pl.ds(b * CHUNK + i * LANES, LANES)] for i in range(CHUNK // LANES)
            ]
            top = tree(jnp.maximum, logits)
            if b:
                old = stat_max[rows, :]
                top = jnp.maximum(top, old)
            total = tree(jnp.add, [jnp.exp2(v - top) for v in logits])
            if b:
                total = total + stat_sum[rows, :] * jnp.exp2(old - top)
            stat_max[rows, :] = top
            stat_sum[rows, :] = total

    log_a = jnp.float32(-math.log2(here * rows_n))
    log_b = jnp.float32(-math.log2(score.shape[1] * cols_n))

    def logit_rows(g):
        rows = pl.ds(g * GROUP, GROUP)
        return rows, [
            score[rows, pl.ds(b * LANES, LANES)] + dual[pl.ds(b, 1), :] for b in range(blocks)
        ]

    def send_image(step):
        for k, p in enumerate(col_peers):
            send(
                image_src.at[step], image_recv.at[step, k],
                image_ssem.at[step], image_rsem.at[step], col_peer(*p),
            )

    def get_image(step):
        drain(image_recv.at[step], image_rsem.at[step])
        return lse_of(
            [image_src[step]] + [image_recv[step, k] for k in range(len(col_peers))]
        )

    def send_first(step):
        dz = lax.rem(z_n - z, z_n)
        for xt in range(x_n):
            dx = lax.rem(xt - x + x_n, x_n)
            send(
                caption_src.at[step], first_recv.at[(dz - 1) * x_n + dx],
                first_ssem, first_rsem, row_peer(dz, dx),
            )

    def send_planes(step, src, of_peer):
        for zt in range(1 if step == ITERS - 1 else 0, z_n):
            dz = lax.rem(zt - z + z_n, z_n)

            @pl.when(dz != 0)
            def _():
                send(
                    src.at[step], z_recv.at[step, dz - 1],
                    z_ssem.at[step], z_rsem.at[step], of_peer(dz, 0),
                )

    def join(step, count, parts):
        drain(z_recv.at[step, pl.ds(0, count)], z_rsem.at[step])
        dual[...] = log_b - lse_of(parts + [z_recv[step, k] for k in range(count)])

    def join_first(parts):
        drain(first_recv, first_rsem)
        dual[...] = log_b - lse_of(parts + [first_recv[k] for k in range(first_recv.shape[0])])

    def exchange_zero(step):
        last = step == ITERS - 1
        if last:
            pl.when(z != 0)(functools.partial(send_first, step))
        for dx in x_peers + [0]:
            send(
                caption_src.at[step], cross_recv.at[step, dx],
                x_ssem.at[step], cross_rsem.at[step], cross_peer(0, dx),
            )

        def normal():
            join(step, z_n, [])

        if not last:
            normal()
            return
        pl.when(z != 0)(normal)

        @pl.when(z == 0)
        def _():
            sibling = z_recv.at[step, z_n - 1]
            drain(sibling, z_rsem.at[step])
            join_first([sibling[...]])

    def exchange_one(step):
        last = step == ITERS - 1
        if last:
            pl.when(z != 0)(functools.partial(send_first, step))
        for dx in x_peers:
            send(
                caption_src.at[step], x_recv.at[step, dx - 1],
                x_ssem.at[step], x_rsem.at[step], row_peer(0, dx),
            )
        drain(x_recv.at[step], x_rsem.at[step])
        plane = lse_of([caption_src[step]] + [x_recv[step, k] for k in range(x_n - 1)])
        plane_src[step] = plane
        send_planes(step, plane_src, row_peer)
        drain(cross_recv.at[step], cross_rsem.at[step])
        cross_src[step] = lse_of([cross_recv[step, k] for k in range(x_n)])
        send_planes(step, cross_src, cross_peer)
        send(
            cross_src.at[step], z_recv.at[step, z_n - 1],
            z_ssem.at[step], z_rsem.at[step], cross_peer(0, 0),
        )

        def normal():
            join(step, z_n - 1, [plane])

        if last:
            pl.when(z != 0)(normal)
            pl.when(z == 0)(functools.partial(join_first, [plane]))
        else:
            normal()

    for step in range(ITERS):
        for g in range(here // GROUP if step else 0):
            rows, logits = logit_rows(g)
            top = tree(jnp.maximum, logits)
            stat_max[rows, :] = top
            stat_sum[rows, :] = tree(jnp.add, [jnp.exp2(v - top) for v in logits])
        lane_max = stat_max[...].T
        top = jnp.max(lane_max, axis=0, keepdims=True)
        total = jnp.sum(stat_sum[...].T * jnp.exp2(lane_max - top), axis=0, keepdims=True)
        image_src[step] = top + jnp.log2(total)
        if step == 0:
            from_zero = x_n - 1 + jnp.where(z == 0, 0, x_n)
            from_one = x_n - 1 + 2 * (z_n - 1) + jnp.where(z == 0, 0, x_n - 1)
            pl.semaphore_wait(barrier, len(col_peers) + jnp.where(core == 0, from_zero, from_one))
        send_image(step)
        image_dual = log_a - get_image(step)
        if step == ITERS - 1:
            image_out[...] = image_dual * jnp.float32(ENTROPIC / LOG2E)
        column = jnp.broadcast_to(image_dual, (LANES, here)).T
        for b in range(blocks):
            block_max[pl.ds(b, 1), :] = jnp.max(
                score[:, pl.ds(b * LANES, LANES)] + column, axis=0, keepdims=True
            )
        for b in range(blocks):
            logits = score[:, pl.ds(b * LANES, LANES)] + column
            block_sum[pl.ds(b, 1), :] = jnp.sum(
                jnp.exp2(logits - block_max[pl.ds(b, 1), :]), axis=0, keepdims=True
            )
        caption_src[step] = block_max[...] + jnp.log2(block_sum[...])
        pl.when(core == 0)(functools.partial(exchange_zero, step))
        pl.when(core != 0)(functools.partial(exchange_one, step))

    caption_out[...] = dual[...] * jnp.float32(ENTROPIC / LOG2E)
    for g in range(here // GROUP):
        rows, logits = logit_rows(g)
        top = jnp.max(tree(jnp.maximum, logits), axis=1, keepdims=True)
        stat_max[rows, :] = jnp.broadcast_to(top, (GROUP, LANES))
        terms = [jnp.exp2(v - top) for v in logits]
        stat_sum[rows, :] = tree(jnp.add, terms)
        for b, w in enumerate(terms):
            weights[rows, pl.ds(b * LANES, LANES)] = w.astype(jnp.bfloat16)
    tail_src[0:1, :] = stat_max[...].T[0:1, :]
    tail_src[1:2, :] = jnp.sum(stat_sum[...].T, axis=0, keepdims=True)

    def chunk(yt, of_core):
        return pl.ds(pl.multiple_of((2 * yt + of_core) * share, 8), share)

    made = set()
    for q, yt in enumerate(y_order):
        for b in range(2 * share * yt // LANES, -(-2 * share * (yt + 1) // LANES)):
            if b not in made:
                made.add(b)
                part = pl.ds(b * LANES, LANES)
                numer[part, :] = jnp.dot(
                    weights[...], captions[:, part], preferred_element_type=jnp.float32
                ).T
        send(
            numer.at[chunk(yt, core)], pair_recv.at[yt],
            pair_ssem, pair_rsem.at[yt], col_peer(0, 1),
        )
        if q == 0:
            tail_recv[c] = tail_src[...]
            send(tail_src, tail_recv.at[c], tail_ssem, tail_rsem.at[0], col_peer(0, 1))
    for p in col_peers[1:]:
        send(tail_src, tail_recv.at[c], tail_ssem, tail_rsem.at[1], col_peer(*p))

    other = tail_recv.at[c + 1 - 2 * core]
    drain(other, tail_rsem.at[0])
    pair_top = jnp.maximum(tail_src[0:1, :], other[0:1, :])
    own_scale = jnp.exp2(tail_src[0:1, :] - pair_top)
    other_scale = jnp.exp2(other[0:1, :] - pair_top)
    for yt in y_order:
        drain(pair_recv.at[yt], pair_rsem.at[yt])
        y_src[yt] = numer[chunk(yt, 1 - core), :] * own_scale + pair_recv[yt] * other_scale
        send(y_src.at[yt], y_recv.at[y], y_ssem, y_rsem, (r, 2 * yt + 1 - core))

    drain(tail_recv.at[pl.ds(0, cols_n - 2)], tail_rsem.at[1])
    tops = [tail_recv[k, 0:1, :] for k in range(cols_n)]
    top = tree(jnp.maximum, tops)
    mass = tree(jnp.add, [tail_recv[k, 1:2, :] * jnp.exp2(tops[k] - top) for k in range(cols_n)])
    inverse = 1.0 / mass
    factor = [
        jnp.exp2(jnp.maximum(tops[2 * k], tops[2 * k + 1]) - top) * inverse for k in range(y_n)
    ]
    drain(y_recv, y_rsem)
    mapped_out[...] = tree(jnp.add, [y_recv[k] * factor[k] for k in range(y_n)])

    drain(tail_recv.at[pl.ds(0, cols_n - 1)], tail_ssem)
    drain(pair_recv, pair_ssem)
    drain(y_recv, y_ssem)
    for step in range(ITERS):
        drain(image_recv.at[step], image_ssem.at[step])

    @pl.when(z != 0)
    def _():
        drain(first_recv.at[pl.ds(0, x_n)], first_ssem)

    @pl.when(core == 0)
    def _():
        for step in range(ITERS):
            drain(cross_recv.at[step], x_ssem.at[step])

    @pl.when(core != 0)
    def _():
        for step in range(ITERS):
            drain(x_recv.at[step], x_ssem.at[step])
        for step in range(ITERS - 1):
            drain(first_recv.at[pl.ds(0, 2 * z_n - 1)], z_ssem.at[step])

        @pl.when(z == 0)
        def _():
            drain(first_recv.at[pl.ds(0, 2 * z_n - 1)], z_ssem.at[ITERS - 1])

        @pl.when(z != 0)
        def _():
            drain(first_recv.at[pl.ds(0, 2 * z_n - 3)], z_ssem.at[ITERS - 1])


def place(image_dual, caption_dual, mapped, image_out, caption_out, mapped_out, sems):
    pairs = ((mapped, mapped_out), (caption_dual, caption_out), (image_dual, image_out))
    copies = [pltpu.make_async_copy(a, b, sems.at[i]) for i, (a, b) in enumerate(pairs)]
    for copy in copies:
        copy.start()
    for copy in copies:
        copy.wait()


def solution(mesh):
    rows_n, cols_n = mesh.shape["row"], mesh.shape["col"]
    y_n = cols_n // 2

    def per_device(images, captions):
        here, width = images.shape
        cols = captions.shape[0]
        share = width // cols_n
        blocks = cols // LANES
        f32 = jnp.float32
        vmem = pl.BlockSpec(memory_space=pltpu.VMEM)
        dma = pltpu.SemaphoreType.DMA
        shapes = ((1, here), (blocks, LANES), (share, here))
        parts = pl.pallas_call(
            functools.partial(kernel, rows_n, cols_n),
            out_shape=tuple(pltpu.VMEM(shape, f32) for shape in shapes),
            in_specs=[pl.BlockSpec(memory_space=pl.ANY)] * 2,
            out_specs=(vmem, vmem, vmem),
            scratch_shapes=[
                pltpu.VMEM((here, width), jnp.bfloat16),
                pltpu.VMEM((cols, width), jnp.bfloat16),
                pltpu.VMEM((here, cols), f32),
                pltpu.VMEM((here, cols), jnp.bfloat16),
                pltpu.VMEM((here, LANES), f32),
                pltpu.VMEM((here, LANES), f32),
                pltpu.VMEM((blocks, LANES), f32),
                pltpu.VMEM((blocks, LANES), f32),
                pltpu.VMEM((blocks, LANES), f32),
                pltpu.VMEM((ITERS, 1, here), f32),
                pltpu.VMEM((ITERS, cols_n - 1, 1, here), f32),
                pltpu.VMEM((ITERS, blocks, LANES), f32),
                pltpu.VMEM((ITERS, X_CHIPS - 1, blocks, LANES), f32),
                pltpu.VMEM((ITERS, X_CHIPS, blocks, LANES), f32),
                pltpu.VMEM((ITERS, blocks, LANES), f32),
                pltpu.VMEM((ITERS, blocks, LANES), f32),
                pltpu.VMEM((ITERS, rows_n // X_CHIPS, blocks, LANES), f32),
                pltpu.VMEM((rows_n - X_CHIPS, blocks, LANES), f32),
                pltpu.VMEM((2, here), f32),
                pltpu.VMEM((cols_n, 2, here), f32),
                pltpu.VMEM((width, here), f32),
                pltpu.VMEM((y_n, share, here), f32),
                pltpu.VMEM((y_n, share, here), f32),
                pltpu.VMEM((y_n, share, here), f32),
                dma((cols // CHUNK + 1,)),
                dma((ITERS,)),
                dma((ITERS,)),
                dma((ITERS,)),
                dma((ITERS,)),
                dma((ITERS,)),
                dma((ITERS,)),
                dma((ITERS,)),
                dma,
                dma,
                dma,
                dma((2,)),
                dma,
                dma((y_n,)),
                dma,
                dma,
            ],
            compiler_params=pltpu.CompilerParams(
                collective_id=0, has_side_effects=True, vmem_limit_bytes=60 * 2**20
            ),
            name="sinkhorn",
        )(images, captions)
        image_dual, caption_dual, mapped = pl.pallas_call(
            place,
            out_shape=tuple(jax.ShapeDtypeStruct(shape, f32) for shape in shapes),
            in_specs=[vmem] * 3,
            out_specs=[pl.BlockSpec(memory_space=pl.ANY)] * 3,
            scratch_shapes=[dma((3,))],
            name="place",
        )(*[pltpu.with_memory_space_constraint(p, pltpu.VMEM) for p in parts])
        return image_dual.reshape(here), caption_dual.reshape(cols), mapped.T

    return jax.shard_map(
        per_device,
        mesh=mesh,
        in_specs=(P("row", None), P("col", None)),
        out_specs=(P("row"), P("col"), P("row", "col")),
        check_vma=False,
    )
```

```python
import functools
import math

import jax
import jax.numpy as jnp
from jax import lax
from jax.experimental import pallas as pl
from jax.experimental.pallas import tpu as pltpu
from jax.sharding import PartitionSpec as P

MESH = pl.DeviceIdType.MESH
ENTROPIC = 0.05
LOG2E = math.log2(math.e)
ITERS = 2
LANES = 128
GROUP = 16
STEP = 8
CHUNK = 512
X_CHIPS = 4


def ring(offset, size):
    return min(offset, size - offset)


def tree(op, values):
    values = list(values)
    while len(values) > 1:
        rest = [op(a, b) for a, b in zip(values[::2], values[1::2])]
        values = rest + ([values[-1]] if len(values) % 2 else [])
    return values[0]


def lse_of(parts):
    top = tree(jnp.maximum, parts)
    return top + jnp.log2(tree(jnp.add, [jnp.exp2(p - top) for p in parts]))


def send(src, dst, ssem, rsem, device):
    pltpu.make_async_remote_copy(
        src_ref=src, dst_ref=dst, send_sem=ssem, recv_sem=rsem,
        device_id=device, device_id_type=MESH,
    ).start()


def drain(ref, sem):
    pltpu.make_async_copy(ref, ref, sem).wait()


def greet(barrier, device):
    pl.semaphore_signal(barrier, inc=1, device_id=device, device_id_type=MESH)


def kernel(
    rows_n, cols_n, images_hbm, captions_hbm, image_out, caption_out, mapped_out,
    images, captions, score, weights, stat_max, stat_sum, block_max, block_sum, dual,
    image_src, image_recv, caption_src, x_recv, cross_recv, plane_src, cross_src, z_recv, first_recv,
    tail_src, tail_recv, numer, pair_recv, y_src, y_recv,
    load_sem, image_ssem, image_rsem, x_ssem, x_rsem, cross_rsem, z_ssem, z_rsem,
    first_ssem, first_rsem, tail_ssem, tail_rsem,
    pair_ssem, pair_rsem, y_ssem, y_rsem,
):
    here, width = images.shape
    blocks = score.shape[1] // LANES
    loads = captions.shape[0] // CHUNK
    x_n = X_CHIPS
    z_n = rows_n // x_n
    y_n = cols_n // 2
    share = width // cols_n
    r, c = lax.axis_index("row"), lax.axis_index("col")
    z, x, y, core = r // x_n, lax.rem(r, x_n), c // 2, lax.rem(c, 2)

    def row_peer(dz, dx):
        return (lax.rem(z + dz, z_n) * x_n + lax.rem(x + dx, x_n), c)

    def cross_peer(dz, dx):
        return (row_peer(dz, dx)[0], c + 1 - 2 * core)

    def col_peer(dy, dc):
        return (r, lax.rem(y + dy, y_n) * 2 + lax.rem(core + dc, 2))

    x_peers = sorted(range(1, x_n), key=lambda p: -ring(p, x_n))
    col_peers = sorted(
        [(dy, dc) for dy in range(y_n) for dc in range(2) if dy or dc],
        key=lambda p: (p[0] > 0, -ring(p[0], y_n), p[1]),
    )
    y_order = list(range(y_n))

    image_load = pltpu.make_async_copy(images_hbm, images, load_sem.at[loads])
    image_load.start()
    caption_loads = []
    for b in range(loads):
        part = pl.ds(b * CHUNK, CHUNK)
        caption_loads.append(
            pltpu.make_async_copy(captions_hbm.at[part], captions.at[part], load_sem.at[b])
        )
        caption_loads[-1].start()

    barrier = pltpu.get_barrier_semaphore()
    z_peers = sorted(range(1, z_n), key=lambda p: -ring(p, z_n))

    @pl.when(core == 0)
    def _():
        for dz in z_peers:
            greet(barrier, cross_peer(dz, 0))

    @pl.when(core != 0)
    def _():
        for dz in z_peers:
            greet(barrier, row_peer(dz, 0))
        for dx in x_peers:
            greet(barrier, row_peer(0, dx))
            greet(barrier, cross_peer(0, dx))

    @pl.when(z == 0)
    def _():
        for dz in z_peers:
            for dx in x_peers:
                greet(barrier, row_peer(dz, dx))

    @pl.when(jnp.logical_and(z == 0, core == 0))
    def _():
        for dz in z_peers:
            greet(barrier, row_peer(dz, 0))

    for p in col_peers:
        greet(barrier, col_peer(*p))

    image_load.wait()
    for b in range(loads):
        caption_loads[b].wait()
        part = pl.ds(b * CHUNK, CHUNK)
        score[:, part] = lax.dot_general(
            images[...], captions[part, :], (((1,), (1,)), ((), ())),
            preferred_element_type=jnp.float32,
        ) * jnp.float32(LOG2E / ENTROPIC)
        for g in range(here // STEP):
            rows = pl.ds(g * STEP, STEP)
            logits = [
                score[rows, pl.ds(b * CHUNK + i * LANES, LANES)] for i in range(CHUNK // LANES)
            ]
            top = tree(jnp.maximum, logits)
            if b:
                old = stat_max[rows, :]
                top = jnp.maximum(top, old)
            total = tree(jnp.add, [jnp.exp2(v - top) for v in logits])
            if b:
                total = total + stat_sum[rows, :] * jnp.exp2(old - top)
            stat_max[rows, :] = top
            stat_sum[rows, :] = total

    log_a = jnp.float32(-math.log2(here * rows_n))
    log_b = jnp.float32(-math.log2(score.shape[1] * cols_n))

    def logit_rows(g, size):
        rows = pl.ds(g * size, size)
        return rows, [
            score[rows, pl.ds(b * LANES, LANES)] + dual[pl.ds(b, 1), :] for b in range(blocks)
        ]

    def send_image(step):
        for k, p in enumerate(col_peers):
            send(
                image_src.at[step], image_recv.at[step, k],
                image_ssem.at[step], image_rsem.at[step], col_peer(*p),
            )

    def get_image(step):
        drain(image_recv.at[step], image_rsem.at[step])
        return lse_of(
            [image_src[step]] + [image_recv[step, k] for k in range(len(col_peers))]
        )

    def send_first(step):
        dz = lax.rem(z_n - z, z_n)
        for xt in range(x_n):
            dx = lax.rem(xt - x + x_n, x_n)
            send(
                caption_src.at[step], first_recv.at[(dz - 1) * x_n + dx],
                first_ssem, first_rsem, row_peer(dz, dx),
            )

    def send_planes(step, src, of_peer):
        for zt in range(1 if step == ITERS - 1 else 0, z_n):
            dz = lax.rem(zt - z + z_n, z_n)

            @pl.when(dz != 0)
            def _():
                send(
                    src.at[step], z_recv.at[step, dz - 1],
                    z_ssem.at[step], z_rsem.at[step], of_peer(dz, 0),
                )

    def join(step, count, parts):
        drain(z_recv.at[step, pl.ds(0, count)], z_rsem.at[step])
        dual[...] = log_b - lse_of(parts + [z_recv[step, k] for k in range(count)])

    def join_first(parts):
        drain(first_recv, first_rsem)
        dual[...] = log_b - lse_of(parts + [first_recv[k] for k in range(first_recv.shape[0])])

    def exchange_zero(step):
        last = step == ITERS - 1
        if last:
            pl.when(z != 0)(functools.partial(send_first, step))
        for dx in x_peers + [0]:
            send(
                caption_src.at[step], cross_recv.at[step, dx],
                x_ssem.at[step], cross_rsem.at[step], cross_peer(0, dx),
            )

        def normal():
            join(step, z_n, [])

        if not last:
            normal()
            return
        pl.when(z != 0)(normal)

        @pl.when(z == 0)
        def _():
            sibling = z_recv.at[step, z_n - 1]
            drain(sibling, z_rsem.at[step])
            join_first([sibling[...]])

    def exchange_one(step):
        last = step == ITERS - 1
        if last:
            pl.when(z != 0)(functools.partial(send_first, step))
        for dx in x_peers:
            send(
                caption_src.at[step], x_recv.at[step, dx - 1],
                x_ssem.at[step], x_rsem.at[step], row_peer(0, dx),
            )
        drain(x_recv.at[step], x_rsem.at[step])
        plane = lse_of([caption_src[step]] + [x_recv[step, k] for k in range(x_n - 1)])
        plane_src[step] = plane
        send_planes(step, plane_src, row_peer)
        drain(cross_recv.at[step], cross_rsem.at[step])
        cross_src[step] = lse_of([cross_recv[step, k] for k in range(x_n)])
        send_planes(step, cross_src, cross_peer)
        send(
            cross_src.at[step], z_recv.at[step, z_n - 1],
            z_ssem.at[step], z_rsem.at[step], cross_peer(0, 0),
        )

        def normal():
            join(step, z_n - 1, [plane])

        if last:
            pl.when(z != 0)(normal)
            pl.when(z == 0)(functools.partial(join_first, [plane]))
        else:
            normal()

    for step in range(ITERS):
        for g in range(here // STEP if step else 0):
            rows, logits = logit_rows(g, STEP)
            top = tree(jnp.maximum, logits)
            stat_max[rows, :] = top
            stat_sum[rows, :] = tree(jnp.add, [jnp.exp2(v - top) for v in logits])
        lane_max = stat_max[...].T
        top = jnp.max(lane_max, axis=0, keepdims=True)
        total = jnp.sum(stat_sum[...].T * jnp.exp2(lane_max - top), axis=0, keepdims=True)
        image_src[step] = top + jnp.log2(total)
        if step == 0:
            from_zero = x_n - 1 + jnp.where(z == 0, 0, x_n)
            from_one = x_n - 1 + 2 * (z_n - 1) + jnp.where(z == 0, 0, x_n - 1)
            pl.semaphore_wait(barrier, len(col_peers) + jnp.where(core == 0, from_zero, from_one))
        send_image(step)
        image_dual = log_a - get_image(step)
        if step == ITERS - 1:
            image_out[...] = image_dual * jnp.float32(ENTROPIC / LOG2E)
        column = jnp.broadcast_to(image_dual, (LANES, here)).T
        for b in range(blocks):
            block_max[pl.ds(b, 1), :] = jnp.max(
                score[:, pl.ds(b * LANES, LANES)] + column, axis=0, keepdims=True
            )
        for b in range(blocks):
            logits = score[:, pl.ds(b * LANES, LANES)] + column
            block_sum[pl.ds(b, 1), :] = jnp.sum(
                jnp.exp2(logits - block_max[pl.ds(b, 1), :]), axis=0, keepdims=True
            )
        caption_src[step] = block_max[...] + jnp.log2(block_sum[...])
        pl.when(core == 0)(functools.partial(exchange_zero, step))
        pl.when(core != 0)(functools.partial(exchange_one, step))

    caption_out[...] = dual[...] * jnp.float32(ENTROPIC / LOG2E)
    for g in range(here // GROUP):
        rows, logits = logit_rows(g, GROUP)
        top = jnp.max(tree(jnp.maximum, logits), axis=1, keepdims=True)
        stat_max[rows, :] = jnp.broadcast_to(top, (GROUP, LANES))
        terms = [jnp.exp2(v - top) for v in logits]
        stat_sum[rows, :] = tree(jnp.add, terms)
        for b, w in enumerate(terms):
            weights[rows, pl.ds(b * LANES, LANES)] = w.astype(jnp.bfloat16)
    tail_src[0:1, :] = stat_max[...].T[0:1, :]
    tail_src[1:2, :] = jnp.sum(stat_sum[...].T, axis=0, keepdims=True)

    def chunk(yt, of_core):
        return pl.ds(pl.multiple_of((2 * yt + of_core) * share, 8), share)

    made = set()
    for q, yt in enumerate(y_order):
        for b in range(2 * share * yt // LANES, -(-2 * share * (yt + 1) // LANES)):
            if b not in made:
                made.add(b)
                part = pl.ds(b * LANES, LANES)
                numer[part, :] = jnp.dot(
                    weights[...], captions[:, part], preferred_element_type=jnp.float32
                ).T
        send(
            numer.at[chunk(yt, core)], pair_recv.at[yt],
            pair_ssem, pair_rsem.at[yt], col_peer(0, 1),
        )
        if q == 0:
            tail_recv[c] = tail_src[...]
            send(tail_src, tail_recv.at[c], tail_ssem, tail_rsem.at[0], col_peer(0, 1))
    for p in col_peers[1:]:
        send(tail_src, tail_recv.at[c], tail_ssem, tail_rsem.at[1], col_peer(*p))

    other = tail_recv.at[c + 1 - 2 * core]
    drain(other, tail_rsem.at[0])
    pair_top = jnp.maximum(tail_src[0:1, :], other[0:1, :])
    own_scale = jnp.exp2(tail_src[0:1, :] - pair_top)
    other_scale = jnp.exp2(other[0:1, :] - pair_top)
    for yt in y_order:
        drain(pair_recv.at[yt], pair_rsem.at[yt])
        y_src[yt] = numer[chunk(yt, 1 - core), :] * own_scale + pair_recv[yt] * other_scale
        send(y_src.at[yt], y_recv.at[y], y_ssem, y_rsem, (r, 2 * yt + 1 - core))

    drain(tail_recv.at[pl.ds(0, cols_n - 2)], tail_rsem.at[1])
    tops = [tail_recv[k, 0:1, :] for k in range(cols_n)]
    top = tree(jnp.maximum, tops)
    mass = tree(jnp.add, [tail_recv[k, 1:2, :] * jnp.exp2(tops[k] - top) for k in range(cols_n)])
    inverse = 1.0 / mass
    factor = [
        jnp.exp2(jnp.maximum(tops[2 * k], tops[2 * k + 1]) - top) * inverse for k in range(y_n)
    ]
    drain(y_recv, y_rsem)
    mapped_out[...] = tree(jnp.add, [y_recv[k] * factor[k] for k in range(y_n)])

    drain(tail_recv.at[pl.ds(0, cols_n - 1)], tail_ssem)
    drain(pair_recv, pair_ssem)
    drain(y_recv, y_ssem)
    for step in range(ITERS):
        drain(image_recv.at[step], image_ssem.at[step])

    @pl.when(z != 0)
    def _():
        drain(first_recv.at[pl.ds(0, x_n)], first_ssem)

    @pl.when(core == 0)
    def _():
        for step in range(ITERS):
            drain(cross_recv.at[step], x_ssem.at[step])

    @pl.when(core != 0)
    def _():
        for step in range(ITERS):
            drain(x_recv.at[step], x_ssem.at[step])
        for step in range(ITERS - 1):
            drain(first_recv.at[pl.ds(0, 2 * z_n - 1)], z_ssem.at[step])

        @pl.when(z == 0)
        def _():
            drain(first_recv.at[pl.ds(0, 2 * z_n - 1)], z_ssem.at[ITERS - 1])

        @pl.when(z != 0)
        def _():
            drain(first_recv.at[pl.ds(0, 2 * z_n - 3)], z_ssem.at[ITERS - 1])


def place(image_dual, caption_dual, mapped, image_out, caption_out, mapped_out, sems):
    pairs = ((mapped, mapped_out), (caption_dual, caption_out), (image_dual, image_out))
    copies = [pltpu.make_async_copy(a, b, sems.at[i]) for i, (a, b) in enumerate(pairs)]
    for copy in copies:
        copy.start()
    for copy in copies:
        copy.wait()


def solution(mesh):
    rows_n, cols_n = mesh.shape["row"], mesh.shape["col"]
    y_n = cols_n // 2

    def per_device(images, captions):
        here, width = images.shape
        cols = captions.shape[0]
        share = width // cols_n
        blocks = cols // LANES
        f32 = jnp.float32
        vmem = pl.BlockSpec(memory_space=pltpu.VMEM)
        dma = pltpu.SemaphoreType.DMA
        shapes = ((1, here), (blocks, LANES), (share, here))
        parts = pl.pallas_call(
            functools.partial(kernel, rows_n, cols_n),
            out_shape=tuple(pltpu.VMEM(shape, f32) for shape in shapes),
            in_specs=[pl.BlockSpec(memory_space=pl.ANY)] * 2,
            out_specs=(vmem, vmem, vmem),
            scratch_shapes=[
                pltpu.VMEM((here, width), jnp.bfloat16),
                pltpu.VMEM((cols, width), jnp.bfloat16),
                pltpu.VMEM((here, cols), f32),
                pltpu.VMEM((here, cols), jnp.bfloat16),
                pltpu.VMEM((here, LANES), f32),
                pltpu.VMEM((here, LANES), f32),
                pltpu.VMEM((blocks, LANES), f32),
                pltpu.VMEM((blocks, LANES), f32),
                pltpu.VMEM((blocks, LANES), f32),
                pltpu.VMEM((ITERS, 1, here), f32),
                pltpu.VMEM((ITERS, cols_n - 1, 1, here), f32),
                pltpu.VMEM((ITERS, blocks, LANES), f32),
                pltpu.VMEM((ITERS, X_CHIPS - 1, blocks, LANES), f32),
                pltpu.VMEM((ITERS, X_CHIPS, blocks, LANES), f32),
                pltpu.VMEM((ITERS, blocks, LANES), f32),
                pltpu.VMEM((ITERS, blocks, LANES), f32),
                pltpu.VMEM((ITERS, rows_n // X_CHIPS, blocks, LANES), f32),
                pltpu.VMEM((rows_n - X_CHIPS, blocks, LANES), f32),
                pltpu.VMEM((2, here), f32),
                pltpu.VMEM((cols_n, 2, here), f32),
                pltpu.VMEM((width, here), f32),
                pltpu.VMEM((y_n, share, here), f32),
                pltpu.VMEM((y_n, share, here), f32),
                pltpu.VMEM((y_n, share, here), f32),
                dma((cols // CHUNK + 1,)),
                dma((ITERS,)),
                dma((ITERS,)),
                dma((ITERS,)),
                dma((ITERS,)),
                dma((ITERS,)),
                dma((ITERS,)),
                dma((ITERS,)),
                dma,
                dma,
                dma,
                dma((2,)),
                dma,
                dma((y_n,)),
                dma,
                dma,
            ],
            compiler_params=pltpu.CompilerParams(
                collective_id=0, has_side_effects=True, vmem_limit_bytes=60 * 2**20
            ),
            name="sinkhorn",
        )(images, captions)
        image_dual, caption_dual, mapped = pl.pallas_call(
            place,
            out_shape=tuple(jax.ShapeDtypeStruct(shape, f32) for shape in shapes),
            in_specs=[vmem] * 3,
            out_specs=[pl.BlockSpec(memory_space=pl.ANY)] * 3,
            scratch_shapes=[dma((3,))],
            name="place",
        )(*[pltpu.with_memory_space_constraint(p, pltpu.VMEM) for p in parts])
        return image_dual.reshape(here), caption_dual.reshape(cols), mapped.T

    return jax.shard_map(
        per_device,
        mesh=mesh,
        in_specs=(P("row", None), P("col", None)),
        out_specs=(P("row"), P("col"), P("row", "col")),
        check_vma=False,
    )
```
